32 devices in a mesh: groups: 2 (over y), blk: 4 (over z), kv: 2 (over x), pair: 2 (over core).
Axes of the slice: x: 2, y: 2, z: 4, core: 2. Of those that a mesh axis runs over, the one named last changes fastest.
Arguments:
- queries: bfloat16 [128, 128, 128], P(('groups', 'blk'), ('kv', 'pair')), parts along dimension 0, may hold values from -15 to 15
- root_keys: bfloat16 [16384, 8, 128], P(('groups', 'blk', 'pair'), 'kv'), parts along dimension 0, may hold values from -4 to 4
- root_values: bfloat16 [16384, 8, 128], P(('groups', 'blk', 'pair'), 'kv'), parts along dimension 0, may hold values from -6 to 6
- branch_keys: bfloat16 [16, 2048, 8, 128], P(('groups', 'blk'), 'pair', 'kv'), parts along dimension 0, may hold values from -4 to 4
- branch_values: bfloat16 [16, 2048, 8, 128], P(('groups', 'blk'), 'pair', 'kv'), parts along dimension 0, may hold values from -6 to 6
- request_branch: int32 [128], P(('groups', 'blk')), parts along dimension 0, may hold values from 0 to 7, as said below
- seen_tokens: int32 [128], P(('groups', 'blk')), parts along dimension 0, may hold values from 1 to 2048, as said below
Outputs:
- attended: bfloat16 [128, 128, 128], P(('groups', 'blk'), ('kv', 'pair')), parts along dimension 0
The draws below stay inside these ranges and needn't reach their ends.
There are 2 independent parts, one for each index of `groups`. The reference program is written for one: setup_inputs(seed, part) draws one part's arguments, and reference() takes and returns one part's arrays. A program takes and returns all parts, laid end to end along the dimension named above; each array names one. Nothing has to cross between parts.
Inputs may be any that keep to these rules, and one draw needn't show every extreme that they name: Within a part, request r belongs to one of the 2 branches stored on its own index of blk: request_branch[r] // 2 == r // 16, with r and the branch counted within the part. Every branch has at least one request. `seen_tokens`: on every index of blk some request sees all 2048 positions of its branch.
All inputs are finite; a program needn't handle non-finite values.
Results may differ from the reference program's by a relative error of at most 0.04.
Values may be sent and summed in bfloat16 or wider, within the bound.
No kernel may reach another device: no remote copies, remote signals or barrier semaphores. Data moves between devices by JAX's collectives and lax.ppermute only.
A program may use at most 64 MiB of HBM per device.

```python
import jax
import jax.numpy as jnp
from jax import lax

H = 128
KVH = 8
HD = 128
REQ_DEV = 16
BR_DEV = 2
REQ = 64
BRANCHES = 8
ROOT = 8192
BLEN = 2048


def draw_queries(key, part):
    result = 3.0 * jax.random.truncated_normal(key, -5.0, 5.0, (REQ, H, HD), jnp.float32)
    return result.astype(jnp.bfloat16)


def draw_root_keys(key, part):
    draw_key = jax.random.fold_in(key, 31)
    result = jax.random.truncated_normal(draw_key, -4.0, 4.0, (ROOT, KVH, HD), jnp.float32)
    return result.astype(jnp.bfloat16)


def draw_branch_keys(key, part):
    draw_key = jax.random.fold_in(key, 37)
    result = jax.random.truncated_normal(draw_key, -4.0, 4.0, (BRANCHES, BLEN, KVH, HD), jnp.float32)
    return result.astype(jnp.bfloat16)


def shuffled_slots(key, blocks):
    seeds = jax.random.split(key, blocks)
    return jax.vmap(lambda seed_key: jax.random.permutation(seed_key, REQ_DEV))(seeds)


def draw_request_branch(key, part):
    blocks = REQ // REQ_DEV
    order = shuffled_slots(jax.random.fold_in(key, 11), blocks)
    extra = jax.random.randint(jax.random.fold_in(key, 12), (blocks, REQ_DEV), 0, BR_DEV)
    local = jnp.where(order < BR_DEV, order, extra)
    return (local + BR_DEV * jnp.arange(blocks)[:, None]).reshape(REQ).astype(jnp.int32)


def draw_seen_tokens(key, part):
    blocks = REQ // REQ_DEV
    order = shuffled_slots(jax.random.fold_in(key, 21), blocks)
    lengths = jax.random.randint(jax.random.fold_in(key, 22), (blocks, REQ_DEV), 1, BLEN + 1)
    return jnp.where(order == 0, BLEN, lengths).reshape(REQ).astype(jnp.int32)


def levels(stream_key, shape, cuts, low, top_value):
    loudness, own = 1.0, jax.random.fold_in(stream_key, 6)
    for axis_at, shards_of in cuts:
        draws = jnp.exp(jax.random.uniform(jax.random.fold_in(own, axis_at), (shards_of,), jnp.float32, low / len(cuts), top_value / len(cuts)))
        loudness = loudness * jnp.repeat(draws, shape[axis_at] // shards_of).reshape([-1 if axis == axis_at else 1 for axis in range(len(shape))])
    return loudness


def noise(rng, extent, scale, most, shards=(), held_as=jnp.bfloat16):
    level = levels(rng, extent, shards, -0.22, 0.18) if shards else 1.0
    entries = jax.random.normal(rng, extent, jnp.float32) * scale * level
    return jnp.minimum(jnp.maximum(entries, -most), most).astype(held_as)


def setup_inputs(seed: int = 0, part: int = 0) -> dict:
    splits = jax.random.split(jax.random.key(seed), 8)
    own_keys = jax.random.split(jax.random.fold_in(splits[7], part), 8)
    queries = draw_queries(jax.random.fold_in(jax.random.fold_in(splits[7], part), 71), part)
    root_keys = draw_root_keys(jax.random.fold_in(jax.random.fold_in(splits[7], part), 71), part)
    root_values = noise(own_keys[2], (ROOT, KVH, HD), 1.0, 6.0, ((0, 8), (1, 2)))
    branch_keys = draw_branch_keys(jax.random.fold_in(jax.random.fold_in(splits[7], part), 71), part)
    branch_values = noise(own_keys[4], (BRANCHES, BLEN, KVH, HD), 1.0, 6.0, ((0, 4), (1, 2), (2, 2)))
    request_branch = draw_request_branch(jax.random.fold_in(jax.random.fold_in(splits[7], part), 71), part)
    seen_tokens = draw_seen_tokens(jax.random.fold_in(jax.random.fold_in(splits[7], part), 71), part)
    return {"queries": queries, "root_keys": root_keys, "root_values": root_values, "branch_keys": branch_keys, "branch_values": branch_values, "request_branch": request_branch, "seen_tokens": seen_tokens}


def reference(queries, root_keys, root_values, branch_keys, branch_values, request_branch, seen_tokens):
    group_size = H // KVH
    score_scale = 1.0 / (HD ** 0.5)
    keys_wide = root_keys.astype(jnp.float32)
    values_wide = root_values.astype(jnp.float32)
    positions = jnp.arange(BLEN, dtype=jnp.int32)

    def one_request(request_items):
        query_row, branch_id, seen_count = request_items
        query_heads = query_row.astype(jnp.float32).reshape(KVH, group_size, HD)
        keys_own = lax.dynamic_index_in_dim(branch_keys, branch_id.astype(jnp.int32), 0, keepdims=False).astype(jnp.float32)
        values_own = lax.dynamic_index_in_dim(branch_values, branch_id.astype(jnp.int32), 0, keepdims=False).astype(jnp.float32)
        scores_root = jnp.einsum("kgd,tkd->kgt", query_heads, keys_wide) * score_scale
        scores_branch = jnp.einsum("kgd,tkd->kgt", query_heads, keys_own) * score_scale
        visible = positions < seen_count
        scores_branch = jnp.where(visible, scores_branch, -1.0e30)
        largest = jnp.maximum(jnp.max(scores_root, axis=-1), jnp.max(scores_branch, axis=-1))
        weights_root = jnp.exp(scores_root - largest[..., None])
        weights_branch = jnp.where(visible, jnp.exp(scores_branch - largest[..., None]), 0.0)
        totals = jnp.sum(weights_root, axis=-1) + jnp.sum(weights_branch, axis=-1)
        rounded_root = lax.optimization_barrier(weights_root.astype(jnp.bfloat16)).astype(jnp.float32)
        rounded_branch = lax.optimization_barrier(weights_branch.astype(jnp.bfloat16)).astype(jnp.float32)
        weighted = jnp.einsum("kgt,tkd->kgd", rounded_root, values_wide)
        weighted = weighted + jnp.einsum("kgt,tkd->kgd", rounded_branch, values_own)
        return (weighted / totals[..., None]).astype(jnp.bfloat16).reshape(H, HD)

    return lax.map(one_request, (queries, request_branch, seen_tokens))
```

```python
import functools
import math

import jax
import jax.numpy as jnp
from jax import lax
from jax.experimental import pallas as pl
from jax.experimental.pallas import tpu as pltpu
from jax.sharding import PartitionSpec as P

masked_floor = -1e30
lowest_reference = -1e29
lane_count = 128
stat_pieces = 3
vmem_grant = 40 * 2**20


def vmem_spec():
    return pl.BlockSpec(memory_space=pltpu.VMEM)


def smem_spec():
    return pl.BlockSpec(memory_space=pltpu.SMEM)


def kernel_params():
    return pltpu.CompilerParams(vmem_limit_bytes=vmem_grant)


def exchange(value, axis, apart):
    return lax.ppermute(value, axis, [(i, i ^ apart) for i in range(lax.axis_size(axis))])


def stat_rows(rows):
    return -(-stat_pieces * (rows // lane_count) // 16) * 16


def identity_mask():
    shape = (lane_count, lane_count)
    return lax.broadcasted_iota(jnp.int32, shape, 0) == lax.broadcasted_iota(jnp.int32, shape, 1)


def column_to_rows(column, same):
    pieces = []
    for start in range(0, column.shape[0], lane_count):
        wide = jnp.broadcast_to(column[start : start + lane_count], (lane_count, lane_count))
        pieces.append(jnp.sum(jnp.where(same, wide, 0.0), axis=0, keepdims=True))
    return pieces


def rows_to_column(pieces, same):
    columns = []
    for piece in pieces:
        wide = jnp.broadcast_to(piece, (lane_count, lane_count))
        columns.append(jnp.sum(jnp.where(same, wide, 0.0), axis=1, keepdims=True))
    return jnp.concatenate(columns, axis=0)


def split_stat(value):
    pieces = []
    for _ in range(stat_pieces):
        piece = value.astype(jnp.bfloat16)
        pieces.append(piece)
        value = value - piece.astype(jnp.float32)
    return pieces


def attend(query, keys, values, scale, thresholds=None):
    scores = lax.dot_general(
        query, keys, (((1,), (1,)), ((), ())), preferred_element_type=jnp.float32
    )
    if thresholds is not None:
        slots = lax.broadcasted_iota(jnp.int32, scores.shape, 1)
        scores = jnp.where(slots < thresholds, scores, masked_floor)
    largest = jnp.max(scores, axis=1, keepdims=True)
    if thresholds is not None:
        largest = jnp.maximum(largest, lowest_reference)
    weights = jnp.exp2((scores - largest) * scale)
    totals = jnp.sum(weights, axis=1, keepdims=True)
    sums = jnp.dot(weights.astype(jnp.bfloat16), values, preferred_element_type=jnp.float32)
    return sums, largest * scale, totals


def normalised(sums, largest, totals):
    some = totals > 0.0
    safe = jnp.where(some, totals, 1.0)
    level = jnp.where(some, largest + jnp.log2(safe), masked_floor)
    return sums * (1.0 / safe), level


def store_packed(out_ref, heads, requests, group_size, outs, levels, same):
    rows = requests * heads * group_size
    per_head = requests * group_size
    all_rows = []
    for h in range(heads):
        block = outs[h].astype(jnp.bfloat16).reshape(requests, group_size, lane_count)
        for r in range(requests):
            out_ref[pl.ds((r * heads + h) * group_size, group_size), :] = block[r]
        all_rows += column_to_rows(levels[h], same)
    stats = jnp.concatenate(all_rows, axis=0)
    pieces = [piece.astype(jnp.float32) for piece in split_stat(stats)]
    spare = stat_rows(rows) - stat_pieces * stats.shape[0]
    if spare:
        pieces.append(jnp.zeros((spare, lane_count), jnp.float32))
    out_ref[pl.ds(rows, stat_rows(rows)), :] = jnp.concatenate(pieces, axis=0).astype(jnp.bfloat16)


def load_packed(in_ref, heads, requests, group_size, same):
    rows = requests * heads * group_size
    lines = rows // lane_count
    per_head = lines // heads
    stats = in_ref[pl.ds(rows, stat_rows(rows)), :].astype(jnp.float32)
    joined = stats[:lines]
    for piece in range(1, stat_pieces):
        joined = joined + stats[piece * lines : (piece + 1) * lines]
    outs, levels = [], []
    for h in range(heads):
        parts = [
            in_ref[pl.ds((r * heads + h) * group_size, group_size), :] for r in range(requests)
        ]
        outs.append(jnp.concatenate(parts, axis=0).astype(jnp.float32))
        lines_here = [joined[h * per_head + i : h * per_head + i + 1] for i in range(per_head)]
        levels.append(rows_to_column(lines_here, same))
    return outs, levels


def head_queries(query_ref, head, group_size):
    block = query_ref[:, head * group_size : (head + 1) * group_size, :]
    return block.reshape(block.shape[0] * group_size, block.shape[2])


def split_heads(source_ref, target_ref, first, heads, base, chunk):
    tokens = source_ref.shape[0]

    @pl.loop(0, tokens // chunk)
    def _(step):
        block = source_ref[pl.ds(step * chunk, chunk)]
        block = jnp.swapaxes(block[:, first : first + heads, :], 0, 1)
        target_ref[:, pl.ds(base + step * chunk, chunk), :] = block


def prepare_kernel(pair_ref, ko_ref, vo_ref, kp_ref, vp_ref, k_ref, v_ref):
    tokens, shared, _ = ko_ref.shape
    heads = k_ref.shape[0]
    for choice in range(shared // heads):

        @pl.when(pair_ref[0] == choice)
        def _():
            for base, keys, values in ((0, ko_ref, vo_ref), (tokens, kp_ref, vp_ref)):
                split_heads(keys, k_ref, choice * heads, heads, base, 64)
                split_heads(values, v_ref, choice * heads, heads, base, 64)


def prepare(pair_index, keys, values, other_keys, other_values, heads):
    tokens, _, width = keys.shape
    shape = jax.ShapeDtypeStruct((heads, 2 * tokens, width), keys.dtype)
    return pl.pallas_call(
        prepare_kernel,
        out_shape=(shape, shape),
        in_specs=[smem_spec()] + [vmem_spec()] * 4,
        out_specs=(vmem_spec(), vmem_spec()),
        compiler_params=kernel_params(),
        cost_estimate=pl.CostEstimate(flops=0, bytes_accessed=8 * 2**20, transcendentals=0),
        name="root_prepare",
    )(pair_index, keys, values, other_keys, other_values)


def root_kernel(scale, group_size, query_ref, k_ref, v_ref, out_ref):
    heads = k_ref.shape[0]
    requests = query_ref.shape[0]
    same = identity_mask()
    outs, levels = [], []
    for h in range(heads):
        query = head_queries(query_ref, h, group_size)
        out, level = normalised(*attend(query, k_ref[h], v_ref[h], scale))
        outs.append(out)
        levels.append(level)
    store_packed(out_ref, heads, requests, group_size, outs, levels, same)


def root_block(query, keys, values, scale):
    requests, local_heads, width = query.shape
    heads, tokens, _ = keys.shape
    rows = requests * local_heads
    return pl.pallas_call(
        functools.partial(root_kernel, scale, local_heads // heads),
        out_shape=jax.ShapeDtypeStruct((rows + stat_rows(rows), width), query.dtype),
        in_specs=[vmem_spec()] * 3,
        out_specs=vmem_spec(),
        compiler_params=kernel_params(),
        cost_estimate=pl.CostEstimate(
            flops=4 * rows * tokens * width, bytes_accessed=6 * 2**20, transcendentals=rows * tokens
        ),
        name="root_block",
    )(query, keys, values)


def branch_kernel(
    scale, group_size, pair_ref, branch_ref, seen_ref, mine_ref, theirs_ref, bk_ref, bv_ref,
    mine_out, theirs_out, k_ref, v_ref, limit_ref,
):
    requests, local_heads, _ = mine_ref.shape
    branches, tokens, shared, _ = bk_ref.shape
    heads = local_heads // group_size
    pair = pair_ref[0]
    same = identity_mask()
    for b in range(branches):
        split_heads(bk_ref.at[b], k_ref.at[b], 0, shared, 0, 64)
        split_heads(bv_ref.at[b], v_ref.at[b], 0, shared, 0, 64)
        for r in range(requests):
            here = branch_ref[r] % branches == b
            limit = jnp.where(here, seen_ref[r] - pair * tokens, 0)
            limit_ref[b, pl.ds(r * group_size, group_size), :] = jnp.full(
                (group_size, lane_count), limit, jnp.int32
            )
    for query_ref, out_ref, owner in ((mine_ref, mine_out, pair), (theirs_ref, theirs_out, 1 - pair)):
        outs, levels = [], []
        for h in range(heads):
            query = head_queries(query_ref, h, group_size)
            parts = []
            for b in range(branches):
                keys = k_ref[b, owner * heads + h]
                values = v_ref[b, owner * heads + h]
                parts.append(attend(query, keys, values, scale, limit_ref[b][:, :1]))
            sums, largest, totals = parts[0]
            for other_sums, other_largest, other_totals in parts[1:]:
                top = jnp.maximum(largest, other_largest)
                one, two = jnp.exp2(largest - top), jnp.exp2(other_largest - top)
                sums = sums * one + other_sums * two
                totals = totals * one + other_totals * two
                largest = top
            out, level = normalised(sums, largest, totals)
            outs.append(out)
            levels.append(level)
        store_packed(out_ref, heads, requests, group_size, outs, levels, same)


def branch_block(pair_index, branch, seen, mine, theirs, keys, values, scale, heads):
    requests, local_heads, width = mine.shape
    branches, tokens, shared, _ = keys.shape
    rows = requests * local_heads
    group_size = local_heads // heads
    shape = jax.ShapeDtypeStruct((rows + stat_rows(rows), width), mine.dtype)
    held = pltpu.VMEM((branches, shared, tokens, width), keys.dtype)
    count = 2 * rows * branches * tokens
    return pl.pallas_call(
        functools.partial(branch_kernel, scale, group_size),
        out_shape=(shape, shape),
        in_specs=[smem_spec()] * 3 + [vmem_spec()] * 4,
        out_specs=(vmem_spec(), vmem_spec()),
        scratch_shapes=[
            held,
            held,
            pltpu.VMEM((branches, requests * group_size, lane_count), jnp.int32),
        ],
        compiler_params=kernel_params(),
        cost_estimate=pl.CostEstimate(
            flops=4 * count * width, bytes_accessed=12 * 2**20, transcendentals=count
        ),
        name="branch_block",
    )(pair_index, branch, seen, mine, theirs, keys, values)


def merge_kernel(last, heads, requests, group_size, *refs):
    ins, out_ref = refs[:-1], refs[-1]
    same = identity_mask()
    loaded = [load_packed(ref, heads, requests, group_size, same) for ref in ins]
    outs, levels = [], []
    for h in range(heads):
        top = loaded[0][1][h]
        for _, level in loaded[1:]:
            top = jnp.maximum(top, level[h])
        sums = totals = 0.0
        for out, level in loaded:
            weight = jnp.exp2(level[h] - top)
            sums = sums + out[h] * weight
            totals = totals + weight
        outs.append(sums * (1.0 / totals))
        levels.append(top + jnp.log2(totals))
    if last:
        for h in range(heads):
            block = outs[h].astype(out_ref.dtype).reshape(requests, group_size, lane_count)
            out_ref[:, h * group_size : (h + 1) * group_size, :] = block
    else:
        store_packed(out_ref, heads, requests, group_size, outs, levels, same)


def merge(parts, last, heads, requests, group_size):
    if last:
        shape = (requests, heads * group_size, lane_count)
    else:
        shape = parts[0].shape
    return pl.pallas_call(
        functools.partial(merge_kernel, last, heads, requests, group_size),
        out_shape=jax.ShapeDtypeStruct(shape, parts[0].dtype),
        in_specs=[vmem_spec()] * len(parts),
        out_specs=vmem_spec(),
        compiler_params=kernel_params(),
        cost_estimate=pl.CostEstimate(flops=0, bytes_accessed=2**20, transcendentals=0),
        name="merge_last" if last else "merge_some",
    )(*parts)


def local(queries, root_keys, root_values, branch_keys, branch_values, request_branch, seen_tokens):
    requests, local_heads, width = queries.shape
    shared = root_keys.shape[1]
    blocks = lax.axis_size("blk")
    heads = shared // lax.axis_size("pair")
    group_size = local_heads // heads
    scale = math.log2(math.e) / math.sqrt(width)
    pair_index = lax.axis_index("pair").astype(jnp.int32).reshape(1)

    other_keys = exchange(root_keys, "pair", 1)
    other_values = exchange(root_values, "pair", 1)
    other_queries = exchange(queries, "pair", 1)
    arrived = {}
    for apart in range(blocks - 1, 0, -2):
        arrived[apart] = exchange(queries, "blk", apart)
    for apart in range(blocks - 1, 2, -2):
        arrived[apart ^ 1] = exchange(arrived[apart], "blk", 1)

    keys, values = prepare(pair_index, root_keys, root_values, other_keys, other_values, heads)
    near = [root_block(queries, keys, values, scale)]
    returned = {}
    for apart in arrived:
        returned[apart] = exchange(root_block(arrived[apart], keys, values, scale), "blk", apart)
    mine, theirs = branch_block(
        pair_index, request_branch, seen_tokens, queries, other_queries,
        branch_keys, branch_values, scale, heads,
    )
    near += [mine, exchange(theirs, "pair", 1)]
    order = list(returned)
    near += [returned[apart] for apart in order[:-1]]
    most = merge(near, False, heads, requests, group_size)
    return merge([most, returned[order[-1]]], True, heads, requests, group_size)


def solution(mesh):
    in_specs = (
        P(("groups", "blk"), ("kv", "pair"), None),
        P(("groups", "blk", "pair"), "kv", None),
        P(("groups", "blk", "pair"), "kv", None),
        P(("groups", "blk"), "pair", "kv", None),
        P(("groups", "blk"), "pair", "kv", None),
        P(("groups", "blk")),
        P(("groups", "blk")),
    )
    out_specs = P(("groups", "blk"), ("kv", "pair"), None)
    return jax.shard_map(local, mesh=mesh, in_specs=in_specs, out_specs=out_specs, check_vma=False)
```

```python
import functools
import math

import jax
import jax.numpy as jnp
from jax import lax
from jax.experimental import pallas as pl
from jax.experimental.pallas import tpu as pltpu
from jax.sharding import PartitionSpec as P

masked_floor = -1e30
lowest_reference = -1e29
lane_count = 128
stat_pieces = 3
vmem_grant = 40 * 2**20
branch_grant = 58 * 2**20
chunk_tokens = 256


def vmem_spec():
    return pl.BlockSpec(memory_space=pltpu.VMEM)


def smem_spec():
    return pl.BlockSpec(memory_space=pltpu.SMEM)


def any_specs(operands):
    return [pl.BlockSpec(memory_space=pl.ANY)] * len(operands)


def ordered(kernel, after):
    return lambda *refs: kernel(*refs[len(after) :])


def light_cost():
    return pl.CostEstimate(flops=1, bytes_accessed=1, transcendentals=0)


def kernel_params(grant=vmem_grant):
    return pltpu.CompilerParams(vmem_limit_bytes=grant)


def exchange(value, axis, apart):
    return lax.ppermute(value, axis, [(i, i ^ apart) for i in range(lax.axis_size(axis))])


def stat_rows(rows):
    return -(-stat_pieces * (rows // lane_count) // 16) * 16


def identity_mask():
    shape = (lane_count, lane_count)
    return lax.broadcasted_iota(jnp.int32, shape, 0) == lax.broadcasted_iota(jnp.int32, shape, 1)


def column_to_rows(column, same):
    pieces = []
    for start in range(0, column.shape[0], lane_count):
        wide = jnp.broadcast_to(column[start : start + lane_count], (lane_count, lane_count))
        pieces.append(jnp.sum(jnp.where(same, wide, 0.0), axis=0, keepdims=True))
    return pieces


def rows_to_column(pieces, same):
    columns = []
    for piece in pieces:
        wide = jnp.broadcast_to(piece, (lane_count, lane_count))
        columns.append(jnp.sum(jnp.where(same, wide, 0.0), axis=1, keepdims=True))
    return jnp.concatenate(columns, axis=0)


def split_stat(value):
    pieces = []
    for _ in range(stat_pieces):
        piece = value.astype(jnp.bfloat16)
        pieces.append(piece)
        value = value - piece.astype(jnp.float32)
    return pieces


def attend(query, keys, values, scale, thresholds=None):
    scores = lax.dot_general(
        query, keys, (((1,), (1,)), ((), ())), preferred_element_type=jnp.float32
    )
    if thresholds is not None:
        slots = lax.broadcasted_iota(jnp.int32, scores.shape, 1)
        scores = jnp.where(slots < thresholds, scores, masked_floor)
    largest = jnp.max(scores, axis=1, keepdims=True)
    if thresholds is not None:
        largest = jnp.maximum(largest, lowest_reference)
    weights = jnp.exp2((scores - largest) * scale)
    totals = jnp.sum(weights, axis=1, keepdims=True)
    sums = jnp.dot(weights.astype(jnp.bfloat16), values, preferred_element_type=jnp.float32)
    return sums, largest * scale, totals


def normalised(sums, largest, totals):
    some = totals > 0.0
    safe = jnp.where(some, totals, 1.0)
    level = jnp.where(some, largest + jnp.log2(safe), masked_floor)
    return sums * (1.0 / safe), level


def store_packed(out_ref, heads, requests, group_size, outs, levels, same):
    rows = requests * heads * group_size
    per_head = requests * group_size
    all_rows = []
    for h in range(heads):
        block = outs[h].astype(jnp.bfloat16).reshape(requests, group_size, lane_count)
        for r in range(requests):
            out_ref[pl.ds((r * heads + h) * group_size, group_size), :] = block[r]
        all_rows += column_to_rows(levels[h], same)
    stats = jnp.concatenate(all_rows, axis=0)
    pieces = [piece.astype(jnp.float32) for piece in split_stat(stats)]
    spare = stat_rows(rows) - stat_pieces * stats.shape[0]
    if spare:
        pieces.append(jnp.zeros((spare, lane_count), jnp.float32))
    out_ref[pl.ds(rows, stat_rows(rows)), :] = jnp.concatenate(pieces, axis=0).astype(jnp.bfloat16)


def load_packed(in_ref, heads, requests, group_size, same):
    rows = requests * heads * group_size
    lines = rows // lane_count
    per_head = lines // heads
    stats = in_ref[pl.ds(rows, stat_rows(rows)), :].astype(jnp.float32)
    joined = stats[:lines]
    for piece in range(1, stat_pieces):
        joined = joined + stats[piece * lines : (piece + 1) * lines]
    outs, levels = [], []
    for h in range(heads):
        parts = [
            in_ref[pl.ds((r * heads + h) * group_size, group_size), :] for r in range(requests)
        ]
        outs.append(jnp.concatenate(parts, axis=0).astype(jnp.float32))
        lines_here = [joined[h * per_head + i : h * per_head + i + 1] for i in range(per_head)]
        levels.append(rows_to_column(lines_here, same))
    return outs, levels


def head_queries(query_ref, head, group_size):
    block = query_ref[:, head * group_size : (head + 1) * group_size, :]
    return block.reshape(block.shape[0] * group_size, block.shape[2])


def split_heads(source_ref, target_ref, wide_ref, shared, first, heads, base):
    tokens = source_ref.shape[0] // shared
    chunk = wide_ref.shape[0] // shared

    @pl.loop(0, tokens // chunk)
    def _(step):
        start = pl.multiple_of(step * chunk, chunk)
        rows = pl.multiple_of(step * (chunk * shared), chunk * shared)
        wide_ref[...] = source_ref[pl.ds(rows, chunk * shared), :].astype(jnp.float32)
        for h in range(heads):
            picked = wide_ref[pl.ds(first + h, chunk, stride=shared), :]
            target_ref[h, pl.ds(base + start, chunk), :] = picked.astype(target_ref.dtype)


def prepare_kernel(shared, pair_ref, ko_ref, vo_ref, kp_ref, vp_ref, k_ref, v_ref, wide_ref):
    heads, both, _ = k_ref.shape
    first = pair_ref[0] * heads
    for base, keys, values in ((0, ko_ref, vo_ref), (both // 2, kp_ref, vp_ref)):
        split_heads(keys, k_ref, wide_ref, shared, first, heads, base)
        split_heads(values, v_ref, wide_ref, shared, first, heads, base)


def flat(cache):
    *lead, tokens, shared, width = cache.shape
    return cache.reshape(*lead, tokens * shared, width)


def prepare(pair_index, keys, values, other_keys, other_values, heads, after):
    tokens, shared, width = keys.shape
    shape = jax.ShapeDtypeStruct((heads, 2 * tokens, width), keys.dtype)
    return pl.pallas_call(
        ordered(functools.partial(prepare_kernel, shared), after),
        out_shape=(shape, shape),
        in_specs=any_specs(after) + [smem_spec()] + [vmem_spec()] * 4,
        out_specs=(vmem_spec(), vmem_spec()),
        scratch_shapes=[pltpu.VMEM((chunk_tokens * shared, width), jnp.float32)],
        compiler_params=kernel_params(),
        cost_estimate=light_cost(),
        name="root_prepare",
    )(*after, pair_index, flat(keys), flat(values), flat(other_keys), flat(other_values))


def root_kernel(scale, group_size, query_ref, k_ref, v_ref, out_ref):
    heads = k_ref.shape[0]
    requests = query_ref.shape[0]
    same = identity_mask()
    outs, levels = [], []
    for h in range(heads):
        query = head_queries(query_ref, h, group_size)
        out, level = normalised(*attend(query, k_ref[h], v_ref[h], scale))
        outs.append(out)
        levels.append(level)
    store_packed(out_ref, heads, requests, group_size, outs, levels, same)


def root_block(query, keys, values, scale, after):
    requests, local_heads, width = query.shape
    heads, tokens, _ = keys.shape
    rows = requests * local_heads
    return pl.pallas_call(
        ordered(functools.partial(root_kernel, scale, local_heads // heads), after),
        out_shape=jax.ShapeDtypeStruct((rows + stat_rows(rows), width), query.dtype),
        in_specs=any_specs(after) + [vmem_spec()] * 3,
        out_specs=vmem_spec(),
        compiler_params=kernel_params(),
        cost_estimate=light_cost(),
        name="root_block",
    )(*after, query, keys, values)


def branch_kernel(
    scale, group_size, pair_ref, mine_ref, theirs_ref, branch_hbm, seen_hbm, bk_hbm, bv_hbm,
    mine_out, theirs_out, branch_ref, seen_ref, bk_ref, bv_ref, k_ref, v_ref, limit_ref,
    wide_ref, small_sems, large_sems,
):
    requests, local_heads, _ = mine_ref.shape
    branches, shared, tokens, _ = k_ref.shape
    heads = local_heads // group_size
    small = [
        pltpu.make_async_copy(source, target, small_sems.at[i])
        for i, (source, target) in enumerate(
            ((branch_hbm, branch_ref), (seen_hbm, seen_ref))
        )
    ]
    large = [
        [
            pltpu.make_async_copy(source.at[b], target.at[b], large_sems.at[b, i])
            for i, (source, target) in enumerate(((bk_hbm, bk_ref), (bv_hbm, bv_ref)))
        ]
        for b in range(branches)
    ]
    for copy in small + sum(large, []):
        copy.start()
    for copy in small:
        copy.wait()
    pair = pair_ref[0]
    same = identity_mask()
    for b in range(branches):
        for r in range(requests):
            here = branch_ref[r] % branches == b
            limit = jnp.where(here, seen_ref[r] - pair * tokens, 0)
            limit_ref[b, pl.ds(r * group_size, group_size), :] = jnp.full(
                (group_size, lane_count), limit, jnp.int32
            )
    for b in range(branches):
        for copy, source, target in zip(large[b], (bk_ref, bv_ref), (k_ref, v_ref)):
            copy.wait()
            split_heads(source.at[b], target.at[b], wide_ref, shared, 0, shared, 0)
    for query_ref, out_ref, owner in ((mine_ref, mine_out, pair), (theirs_ref, theirs_out, 1 - pair)):
        outs, levels = [], []
        for h in range(heads):
            query = head_queries(query_ref, h, group_size)
            parts = []
            for b in range(branches):
                keys = k_ref[b, owner * heads + h]
                values = v_ref[b, owner * heads + h]
                parts.append(attend(query, keys, values, scale, limit_ref[b][:, :1]))
            sums, largest, totals = parts[0]
            for other_sums, other_largest, other_totals in parts[1:]:
                top = jnp.maximum(largest, other_largest)
                one, two = jnp.exp2(largest - top), jnp.exp2(other_largest - top)
                sums = sums * one + other_sums * two
                totals = totals * one + other_totals * two
                largest = top
            out, level = normalised(sums, largest, totals)
            outs.append(out)
            levels.append(level)
        store_packed(out_ref, heads, requests, group_size, outs, levels, same)


def branch_block(pair_index, branch, seen, mine, theirs, keys, values, scale, heads):
    requests, local_heads, width = mine.shape
    branches, tokens, shared, _ = keys.shape
    rows = requests * local_heads
    group_size = local_heads // heads
    shape = jax.ShapeDtypeStruct((rows + stat_rows(rows), width), mine.dtype)
    raw = pltpu.VMEM((branches, tokens * shared, width), keys.dtype)
    held = pltpu.VMEM((branches, shared, tokens, width), keys.dtype)
    from_hbm = (branch, seen, flat(keys), flat(values))
    return pl.pallas_call(
        functools.partial(branch_kernel, scale, group_size),
        out_shape=(shape, shape),
        in_specs=[smem_spec(), vmem_spec(), vmem_spec()] + [pl.BlockSpec(memory_space=pltpu.HBM)] * len(from_hbm),
        out_specs=(vmem_spec(), vmem_spec()),
        scratch_shapes=[
            pltpu.SMEM(branch.shape, branch.dtype),
            pltpu.SMEM(seen.shape, seen.dtype),
            raw,
            raw,
            held,
            held,
            pltpu.VMEM((branches, requests * group_size, lane_count), jnp.int32),
            pltpu.VMEM((chunk_tokens * shared, width), jnp.float32),
            pltpu.SemaphoreType.DMA((2,)),
            pltpu.SemaphoreType.DMA((branches, 2)),
        ],
        compiler_params=kernel_params(branch_grant),
        cost_estimate=light_cost(),
        name="branch_block",
    )(pair_index, mine, theirs, *from_hbm)


def merge_kernel(last, heads, requests, group_size, *refs):
    ins, out_ref = refs[:-1], refs[-1]
    same = identity_mask()
    loaded = [load_packed(ref, heads, requests, group_size, same) for ref in ins]
    outs, levels = [], []
    for h in range(heads):
        top = loaded[0][1][h]
        for _, level in loaded[1:]:
            top = jnp.maximum(top, level[h])
        sums = totals = 0.0
        for out, level in loaded:
            weight = jnp.exp2(level[h] - top)
            sums = sums + out[h] * weight
            totals = totals + weight
        outs.append(sums * (1.0 / totals))
        levels.append(top + jnp.log2(totals))
    if last:
        for h in range(heads):
            block = outs[h].astype(out_ref.dtype).reshape(requests, group_size, lane_count)
            out_ref[:, h * group_size : (h + 1) * group_size, :] = block
    else:
        store_packed(out_ref, heads, requests, group_size, outs, levels, same)


def merge(parts, last, heads, requests, group_size, after=()):
    if last:
        shape = (requests, heads * group_size, lane_count)
    else:
        shape = parts[0].shape
    return pl.pallas_call(
        ordered(functools.partial(merge_kernel, last, heads, requests, group_size), after),
        out_shape=jax.ShapeDtypeStruct(shape, parts[0].dtype),
        in_specs=any_specs(after) + [vmem_spec()] * len(parts),
        out_specs=vmem_spec(),
        compiler_params=kernel_params(),
        cost_estimate=light_cost(),
        name="merge_last" if last else "merge_some",
    )(*after, *parts)


def local(queries, root_keys, root_values, branch_keys, branch_values, request_branch, seen_tokens):
    requests, local_heads, width = queries.shape
    shared = root_keys.shape[1]
    blocks = lax.axis_size("blk")
    heads = shared // lax.axis_size("pair")
    group_size = local_heads // heads
    scale = math.log2(math.e) / math.sqrt(width)
    pair_index = lax.axis_index("pair").astype(jnp.int32).reshape(1)

    other_keys = exchange(root_keys, "pair", 1)
    other_values = exchange(root_values, "pair", 1)
    other_queries = exchange(queries, "pair", 1)
    arrived = {}
    for apart in range(blocks - 1, 0, -2):
        arrived[apart] = exchange(queries, "blk", apart)

    mine, theirs = branch_block(
        pair_index, request_branch, seen_tokens, queries, other_queries,
        branch_keys, branch_values, scale, heads,
    )
    from_partner = exchange(theirs, "pair", 1)
    direct = list(arrived)
    *held, mine = lax.optimization_barrier((*arrived.values(), mine))
    arrived = dict(zip(direct, held))
    for apart in range(blocks - 1, 2, -2):
        arrived[apart ^ 1] = exchange(arrived[apart], "blk", 1)
    keys, values = prepare(
        pair_index, root_keys, root_values, other_keys, other_values, heads, (mine,)
    )
    partials, previous = {}, ()
    for apart in sorted(arrived, key=lambda a: (a == 1, -a)):
        partials[apart] = root_block(arrived[apart], keys, values, scale, previous)
        previous = (partials[apart],)
    returned = {apart: exchange(partials[apart], "blk", apart) for apart in sorted(partials)}
    own = root_block(queries, keys, values, scale, previous)
    late = [returned.pop(apart) for apart in (2, 1) if apart in returned]
    most = merge([own, mine, from_partner, *returned.values()], False, heads, requests, group_size)
    for part in late[:-1]:
        most = merge([most, part], False, heads, requests, group_size)
    return merge([most, late[-1]], True, heads, requests, group_size)


def solution(mesh):
    in_specs = (
        P(("groups", "blk"), ("kv", "pair"), None),
        P(("groups", "blk", "pair"), "kv", None),
        P(("groups", "blk", "pair"), "kv", None),
        P(("groups", "blk"), "pair", "kv", None),
        P(("groups", "blk"), "pair", "kv", None),
        P(("groups", "blk")),
        P(("groups", "blk")),
    )
    out_specs = P(("groups", "blk"), ("kv", "pair"), None)
    return jax.shard_map(local, mesh=mesh, in_specs=in_specs, out_specs=out_specs, check_vma=False)
```

```python
import functools
import math

import jax
import jax.numpy as jnp
from jax import lax
from jax.experimental import pallas as pl
from jax.experimental.pallas import tpu as pltpu
from jax.sharding import PartitionSpec as P

masked_floor = -1e30
lowest_reference = -1e29
lane_count = 128
stat_pieces = 3
vmem_grant = 24 * 2**20
chunk_tokens = 256
least_total = 2.0**-60
most_total = 2.0**100


def vmem_spec():
    return pl.BlockSpec(memory_space=pltpu.VMEM)


def smem_spec():
    return pl.BlockSpec(memory_space=pltpu.SMEM)


def any_specs(operands):
    return [pl.BlockSpec(memory_space=pl.ANY)] * len(operands)


def ordered(kernel, after):
    return lambda *refs: kernel(*refs[len(after) :])


def light_cost():
    return pl.CostEstimate(flops=1, bytes_accessed=1, transcendentals=0)


def kernel_params(grant=vmem_grant):
    return pltpu.CompilerParams(vmem_limit_bytes=grant)


def exchange(value, axis, apart):
    return lax.ppermute(value, axis, [(i, i ^ apart) for i in range(lax.axis_size(axis))])


def stat_rows(rows):
    return -(-stat_pieces * (rows // lane_count) // 16) * 16


def identity_mask():
    shape = (lane_count, lane_count)
    return lax.broadcasted_iota(jnp.int32, shape, 0) == lax.broadcasted_iota(jnp.int32, shape, 1)


def column_to_rows(column, same):
    pieces = []
    for start in range(0, column.shape[0], lane_count):
        wide = jnp.broadcast_to(column[start : start + lane_count], (lane_count, lane_count))
        pieces.append(jnp.sum(jnp.where(same, wide, 0.0), axis=0, keepdims=True))
    return pieces


def rows_to_column(pieces, same):
    columns = []
    for piece in pieces:
        wide = jnp.broadcast_to(piece, (lane_count, lane_count))
        columns.append(jnp.sum(jnp.where(same, wide, 0.0), axis=1, keepdims=True))
    return jnp.concatenate(columns, axis=0)


def split_stat(value):
    pieces = []
    for _ in range(stat_pieces):
        piece = value.astype(jnp.bfloat16)
        pieces.append(piece)
        value = value - piece.astype(jnp.float32)
    return pieces


def evaluate(pieces, scale, exact):
    state = None
    visible = None
    for query, keys, values, limits in pieces:
        scores = lax.dot_general(
            query, keys, (((1,), (1,)), ((), ())), preferred_element_type=jnp.float32
        )
        seen = None
        if limits is not None:
            seen = lax.broadcasted_iota(jnp.int32, scores.shape, 1) < limits
            some = limits > 0
            visible = some if visible is None else visible | some
        if exact:
            if seen is not None:
                scores = jnp.where(seen, scores, masked_floor)
            largest = jnp.max(scores, axis=1, keepdims=True)
            if seen is not None:
                largest = jnp.maximum(largest, lowest_reference)
            weights = jnp.exp2((scores - largest) * scale)
            largest = largest * scale
        else:
            weights = jnp.exp2(scores * scale)
            if seen is not None:
                weights = jnp.where(seen, weights, 0.0)
        totals = jnp.sum(weights, axis=1, keepdims=True)
        sums = jnp.dot(weights.astype(jnp.bfloat16), values, preferred_element_type=jnp.float32)
        if state is None:
            state = (sums, totals, largest if exact else None)
        elif exact:
            top = jnp.maximum(state[2], largest)
            one, two = jnp.exp2(state[2] - top), jnp.exp2(largest - top)
            state = (state[0] * one + sums * two, state[1] * one + totals * two, top)
        else:
            state = (state[0] + sums, state[1] + totals, None)
    sums, totals, largest = state
    sound = (totals > least_total) & (totals < most_total)
    safe = totals
    if visible is not None:
        sound = sound | jnp.logical_not(visible)
        safe = jnp.where(visible, totals, 1.0)
    level = jnp.log2(safe)
    if exact:
        level = level + largest
    if visible is not None:
        level = jnp.where(visible, level, masked_floor)
    return sums * (1.0 / safe), level, sound


def write_partials(jobs, scale, heads, requests, group_size):
    same = identity_mask()

    def run(exact):
        least = 1.0
        for out_ref, pieces_of in jobs:
            outs, levels = [], []
            for h in range(heads):
                out, level, sound = evaluate(pieces_of(h), scale, exact)
                outs.append(out)
                levels.append(level)
                least = jnp.minimum(least, jnp.where(sound, 1.0, 0.0))
            store_packed(out_ref, heads, requests, group_size, outs, levels, same)
        return jnp.min(least)

    least = run(False)

    @pl.when(least < 0.5)
    def _():
        run(True)


def store_packed(out_ref, heads, requests, group_size, outs, levels, same):
    rows = requests * heads * group_size
    per_head = requests * group_size
    all_rows = []
    for h in range(heads):
        block = outs[h].astype(jnp.bfloat16).reshape(requests, group_size, lane_count)
        for r in range(requests):
            out_ref[pl.ds((r * heads + h) * group_size, group_size), :] = block[r]
        all_rows += column_to_rows(levels[h], same)
    stats = jnp.concatenate(all_rows, axis=0)
    pieces = [piece.astype(jnp.float32) for piece in split_stat(stats)]
    spare = stat_rows(rows) - stat_pieces * stats.shape[0]
    if spare:
        pieces.append(jnp.zeros((spare, lane_count), jnp.float32))
    out_ref[pl.ds(rows, stat_rows(rows)), :] = jnp.concatenate(pieces, axis=0).astype(jnp.bfloat16)


def load_packed(in_ref, heads, requests, group_size, same):
    rows = requests * heads * group_size
    lines = rows // lane_count
    per_head = lines // heads
    stats = in_ref[pl.ds(rows, stat_rows(rows)), :].astype(jnp.float32)
    joined = stats[:lines]
    for piece in range(1, stat_pieces):
        joined = joined + stats[piece * lines : (piece + 1) * lines]
    outs, levels = [], []
    for h in range(heads):
        parts = [
            in_ref[pl.ds((r * heads + h) * group_size, group_size), :] for r in range(requests)
        ]
        outs.append(jnp.concatenate(parts, axis=0).astype(jnp.float32))
        lines_here = [joined[h * per_head + i : h * per_head + i + 1] for i in range(per_head)]
        levels.append(rows_to_column(lines_here, same))
    return outs, levels


def head_queries(query_ref, head, group_size):
    block = query_ref[:, head * group_size : (head + 1) * group_size, :]
    return block.reshape(block.shape[0] * group_size, block.shape[2])


def split_heads(source_ref, target_ref, wide_ref, shared, first, heads, base):
    tokens = source_ref.shape[0] // shared
    chunk = wide_ref.shape[0] // shared

    @pl.loop(0, tokens // chunk)
    def _(step):
        start = pl.multiple_of(step * chunk, chunk)
        rows = pl.multiple_of(step * (chunk * shared), chunk * shared)
        wide_ref[...] = source_ref[pl.ds(rows, chunk * shared), :].astype(jnp.float32)
        for h in range(heads):
            picked = wide_ref[pl.ds(first + h, chunk, stride=shared), :]
            target_ref[h, pl.ds(base + start, chunk), :] = picked.astype(target_ref.dtype)


def flat(cache):
    *lead, tokens, shared, width = cache.shape
    return cache.reshape(*lead, tokens * shared, width)


def packed_shape(query):
    requests, local_heads, width = query.shape
    rows = requests * local_heads
    return jax.ShapeDtypeStruct((rows + stat_rows(rows), width), query.dtype)


def root_pieces(query_ref, k_ref, v_ref, group_size):
    return lambda h: [(head_queries(query_ref, h, group_size), k_ref[h], v_ref[h], None)]


def first_kernel(
    scale, shared, pair_ref, query_ref, ko_ref, vo_ref, kp_ref, vp_ref, k_ref, v_ref, out_ref, wide_ref
):
    heads, both, _ = k_ref.shape
    first = pair_ref[0] * heads
    for base, keys, values in ((0, ko_ref, vo_ref), (both // 2, kp_ref, vp_ref)):
        split_heads(keys, k_ref, wide_ref, shared, first, heads, base)
        split_heads(values, v_ref, wide_ref, shared, first, heads, base)
    requests, local_heads, _ = query_ref.shape
    group_size = local_heads // heads
    pieces = root_pieces(query_ref, k_ref, v_ref, group_size)
    write_partials([(out_ref, pieces)], scale, heads, requests, group_size)


def first_block(pair_index, query, keys, values, other_keys, other_values, scale, heads):
    tokens, shared, width = keys.shape
    shape = jax.ShapeDtypeStruct((heads, 2 * tokens, width), keys.dtype)
    return pl.pallas_call(
        functools.partial(first_kernel, scale, shared),
        out_shape=(shape, shape, packed_shape(query)),
        in_specs=[smem_spec()] + [vmem_spec()] * 5,
        out_specs=(vmem_spec(),) * 3,
        scratch_shapes=[pltpu.VMEM((chunk_tokens * shared, width), jnp.float32)],
        compiler_params=kernel_params(),
        cost_estimate=light_cost(),
        name="first_block",
    )(pair_index, query, flat(keys), flat(values), flat(other_keys), flat(other_values))


def place_kernel(in_ref, out_ref):
    out_ref[0] = in_ref[0]


def place(pair_index):
    return pl.pallas_call(
        place_kernel,
        out_shape=jax.ShapeDtypeStruct(pair_index.shape, pair_index.dtype),
        in_specs=[smem_spec()],
        out_specs=smem_spec(),
        compiler_params=kernel_params(2**20),
        cost_estimate=pl.CostEstimate(flops=10**10, bytes_accessed=1, transcendentals=0),
        name="place",
    )(pair_index)


def root_kernel(scale, count, k_ref, v_ref, *refs):
    heads = k_ref.shape[0]
    requests, local_heads, _ = refs[0].shape
    group_size = local_heads // heads
    jobs = [
        (out_ref, root_pieces(query_ref, k_ref, v_ref, group_size))
        for query_ref, out_ref in zip(refs[:count], refs[count:])
    ]
    write_partials(jobs, scale, heads, requests, group_size)


def root_blocks(queries, keys, values, scale, after):
    return pl.pallas_call(
        ordered(functools.partial(root_kernel, scale, len(queries)), after),
        out_shape=[packed_shape(query) for query in queries],
        in_specs=any_specs(after) + [vmem_spec()] * (2 + len(queries)),
        out_specs=[vmem_spec()] * len(queries),
        compiler_params=kernel_params(),
        cost_estimate=light_cost(),
        name="root_blocks",
    )(*after, keys, values, *queries)


def branch_kernel(
    scale, shared, pair_ref, branch_ref, seen_ref, query_ref, ko_ref, vo_ref, kp_ref, vp_ref,
    out_ref, k_ref, v_ref, limit_ref, wide_ref,
):
    requests, local_heads, _ = query_ref.shape
    branches, heads, both, _ = k_ref.shape
    group_size = local_heads // heads
    pair = pair_ref[0]
    first = pair * heads
    half = both // 2
    for b in range(branches):
        for owner, keys, values in ((pair, ko_ref, vo_ref), (1 - pair, kp_ref, vp_ref)):
            base = pl.multiple_of(owner * half, half)
            split_heads(keys.at[b], k_ref.at[b], wide_ref, shared, first, heads, base)
            split_heads(values.at[b], v_ref.at[b], wide_ref, shared, first, heads, base)
        for r in range(requests):
            limit = jnp.where(branch_ref[r] % branches == b, seen_ref[r], 0)
            limit_ref[b, pl.ds(r * group_size, group_size), :] = jnp.full(
                (group_size, lane_count), limit, jnp.int32
            )

    def pieces(h):
        query = head_queries(query_ref, h, group_size)
        return [
            (query, k_ref[b, h], v_ref[b, h], limit_ref[b][:, :1]) for b in range(branches)
        ]

    write_partials([(out_ref, pieces)], scale, heads, requests, group_size)


def branch_block(pair_index, branch, seen, query, caches, scale, heads, after):
    branches, tokens, shared, width = caches[0].shape
    requests, local_heads, _ = query.shape
    rows = requests * local_heads // heads
    held = pltpu.VMEM((branches, heads, 2 * tokens, width), caches[0].dtype)
    return pl.pallas_call(
        ordered(functools.partial(branch_kernel, scale, shared), after),
        out_shape=packed_shape(query),
        in_specs=any_specs(after) + [smem_spec()] * 3 + [vmem_spec()] * 5,
        out_specs=vmem_spec(),
        scratch_shapes=[
            held,
            held,
            pltpu.VMEM((branches, rows, lane_count), jnp.int32),
            pltpu.VMEM((chunk_tokens * shared, width), jnp.float32),
        ],
        compiler_params=kernel_params(),
        cost_estimate=light_cost(),
        name="branch_block",
    )(*after, pair_index, branch, seen, query, *map(flat, caches))


def merge_kernel(last, heads, requests, group_size, *refs):
    ins, out_ref = refs[:-1], refs[-1]
    same = identity_mask()
    loaded = [load_packed(ref, heads, requests, group_size, same) for ref in ins]
    outs, levels = [], []
    for h in range(heads):
        top = loaded[0][1][h]
        for _, level in loaded[1:]:
            top = jnp.maximum(top, level[h])
        sums = totals = 0.0
        for out, level in loaded:
            weight = jnp.exp2(level[h] - top)
            sums = sums + out[h] * weight
            totals = totals + weight
        outs.append(sums * (1.0 / totals))
        levels.append(top + jnp.log2(totals))
    if last:
        for h in range(heads):
            block = outs[h].astype(out_ref.dtype).reshape(requests, group_size, lane_count)
            out_ref[:, h * group_size : (h + 1) * group_size, :] = block
    else:
        store_packed(out_ref, heads, requests, group_size, outs, levels, same)


def merge(parts, last, heads, requests, group_size, after=()):
    if last:
        shape = (requests, heads * group_size, lane_count)
    else:
        shape = parts[0].shape
    return pl.pallas_call(
        ordered(functools.partial(merge_kernel, last, heads, requests, group_size), after),
        out_shape=jax.ShapeDtypeStruct(shape, parts[0].dtype),
        in_specs=any_specs(after) + [vmem_spec()] * len(parts),
        out_specs=vmem_spec(),
        compiler_params=kernel_params(),
        cost_estimate=light_cost(),
        name="merge_last" if last else "merge_some",
    )(*after, *parts)


def local(queries, root_keys, root_values, branch_keys, branch_values, request_branch, seen_tokens):
    requests, local_heads, width = queries.shape
    shared = root_keys.shape[1]
    blocks = lax.axis_size("blk")
    heads = shared // lax.axis_size("pair")
    group_size = local_heads // heads
    scale = math.log2(math.e) / math.sqrt(width)
    pair_index = place(lax.axis_index("pair").astype(jnp.int32).reshape(1))

    other_keys = exchange(root_keys, "pair", 1)
    other_values = exchange(root_values, "pair", 1)
    direct = range(blocks - 1, 0, -2)
    arrived = [exchange(queries, "blk", apart) for apart in direct]

    keys, values, own = first_block(
        pair_index, queries, root_keys, root_values, other_keys, other_values, scale, heads
    )
    *arrived, own, far_keys, far_values = lax.optimization_barrier(
        (*arrived, own, branch_keys, branch_values)
    )
    other_branch_keys = exchange(far_keys, "pair", 1)
    other_branch_values = exchange(far_values, "pair", 1)
    arrived = dict(zip(direct, arrived))
    for apart in range(blocks - 1, 2, -2):
        arrived[apart ^ 1] = exchange(arrived[apart], "blk", 1)

    groups = [(apart,) for apart in arrived if apart > 2] + [
        tuple(apart for apart in (2, 1) if apart in arrived)
    ]
    returned, previous = {}, ()
    for group in groups:
        partials = root_blocks([arrived[apart] for apart in group], keys, values, scale, previous)
        previous = (partials[0],)
        for apart, partial in zip(group, partials):
            returned[apart] = exchange(partial, "blk", apart)
    branch = branch_block(
        pair_index, request_branch, seen_tokens, queries,
        (branch_keys, branch_values, other_branch_keys, other_branch_values),
        scale, heads, previous,
    )
    last = returned.pop(max(groups[-1]))
    most = merge([own, branch, *returned.values()], False, heads, requests, group_size)
    return merge([most, last], True, heads, requests, group_size)


def solution(mesh):
    in_specs = (
        P(("groups", "blk"), ("kv", "pair"), None),
        P(("groups", "blk", "pair"), "kv", None),
        P(("groups", "blk", "pair"), "kv", None),
        P(("groups", "blk"), "pair", "kv", None),
        P(("groups", "blk"), "pair", "kv", None),
        P(("groups", "blk")),
        P(("groups", "blk")),
    )
    out_specs = P(("groups", "blk"), ("kv", "pair"), None)
    return jax.shard_map(local, mesh=mesh, in_specs=in_specs, out_specs=out_specs, check_vma=False)
```

```python
import functools
import math

import jax
import jax.numpy as jnp
from jax import lax
from jax.experimental import pallas as pl
from jax.experimental.pallas import tpu as pltpu
from jax.sharding import PartitionSpec as P

masked_floor = -1e30
lowest_reference = -1e29
lane_count = 128
stat_pieces = 3
vmem_grant = 24 * 2**20
chunk_tokens = 256
least_total = 2.0**-60
most_total = 2.0**100


def vmem_spec():
    return pl.BlockSpec(memory_space=pltpu.VMEM)


def smem_spec():
    return pl.BlockSpec(memory_space=pltpu.SMEM)


def any_specs(operands):
    return [pl.BlockSpec(memory_space=pl.ANY)] * len(operands)


def ordered(kernel, after):
    return lambda *refs: kernel(*refs[len(after) :])


def light_cost():
    return pl.CostEstimate(flops=1, bytes_accessed=1, transcendentals=0)


def kernel_params(grant=vmem_grant):
    return pltpu.CompilerParams(vmem_limit_bytes=grant)


def exchange(value, axis, apart):
    return lax.ppermute(value, axis, [(i, i ^ apart) for i in range(lax.axis_size(axis))])


def stat_rows(rows):
    return -(-stat_pieces * (rows // lane_count) // 16) * 16


def identity_mask():
    shape = (lane_count, lane_count)
    return lax.broadcasted_iota(jnp.int32, shape, 0) == lax.broadcasted_iota(jnp.int32, shape, 1)


def column_to_rows(column, same):
    pieces = []
    for start in range(0, column.shape[0], lane_count):
        wide = jnp.broadcast_to(column[start : start + lane_count], (lane_count, lane_count))
        pieces.append(jnp.sum(jnp.where(same, wide, 0.0), axis=0, keepdims=True))
    return pieces


def rows_to_column(pieces, same):
    columns = []
    for piece in pieces:
        wide = jnp.broadcast_to(piece, (lane_count, lane_count))
        columns.append(jnp.sum(jnp.where(same, wide, 0.0), axis=1, keepdims=True))
    return jnp.concatenate(columns, axis=0)


def split_stat(value):
    pieces = []
    for _ in range(stat_pieces):
        piece = value.astype(jnp.bfloat16)
        pieces.append(piece)
        value = value - piece.astype(jnp.float32)
    return pieces


def evaluate(pieces, scale, exact):
    state = None
    visible = None
    for query, keys, values, limits in pieces:
        scores = lax.dot_general(
            query, keys, (((1,), (1,)), ((), ())), preferred_element_type=jnp.float32
        )
        seen = None
        if limits is not None:
            seen = lax.broadcasted_iota(jnp.int32, scores.shape, 1) < limits
            some = limits > 0
            visible = some if visible is None else visible | some
        if exact:
            if seen is not None:
                scores = jnp.where(seen, scores, masked_floor)
            largest = jnp.max(scores, axis=1, keepdims=True)
            if seen is not None:
                largest = jnp.maximum(largest, lowest_reference)
            weights = jnp.exp2((scores - largest) * scale)
            largest = largest * scale
        else:
            weights = jnp.exp2(scores * scale)
            if seen is not None:
                weights = jnp.where(seen, weights, 0.0)
        totals = jnp.sum(weights, axis=1, keepdims=True)
        sums = jnp.dot(weights.astype(jnp.bfloat16), values, preferred_element_type=jnp.float32)
        if state is None:
            state = (sums, totals, largest if exact else None)
        elif exact:
            top = jnp.maximum(state[2], largest)
            one, two = jnp.exp2(state[2] - top), jnp.exp2(largest - top)
            state = (state[0] * one + sums * two, state[1] * one + totals * two, top)
        else:
            state = (state[0] + sums, state[1] + totals, None)
    sums, totals, largest = state
    sound = (totals > least_total) & (totals < most_total)
    safe = totals
    if visible is not None:
        sound = sound | jnp.logical_not(visible)
        safe = jnp.where(visible, totals, 1.0)
    level = jnp.log2(safe)
    if exact:
        level = level + largest
    if visible is not None:
        level = jnp.where(visible, level, masked_floor)
    return sums * (1.0 / safe), level, sound


def combine(parts):
    top = parts[0][1]
    for _, level in parts[1:]:
        top = jnp.maximum(top, level)
    sums = totals = 0.0
    for out, level in parts:
        weight = jnp.exp2(level - top)
        sums = sums + out * weight
        totals = totals + weight
    return sums * (1.0 / totals), top + jnp.log2(totals)


def write_partials(jobs, scale, heads, requests, group_size, others=()):
    same = identity_mask()

    loaded = [load_packed(ref, heads, requests, group_size, same) for ref in others]

    def run(exact):
        least = 1.0
        for out_ref, pieces_of in jobs:
            outs, levels = [], []
            for h in range(heads):
                out, level, sound = evaluate(pieces_of(h), scale, exact)
                if others:
                    added = [(o[h], l[h]) for o, l in loaded]
                    out, level = combine([(out, level), *added])
                outs.append(out)
                levels.append(level)
                least = jnp.minimum(least, jnp.where(sound, 1.0, 0.0))
            store_packed(out_ref, heads, requests, group_size, outs, levels, same)
        return jnp.min(least)

    least = run(False)

    @pl.when(least < 0.5)
    def _():
        run(True)


def store_packed(out_ref, heads, requests, group_size, outs, levels, same):
    rows = requests * heads * group_size
    per_head = requests * group_size
    all_rows = []
    for h in range(heads):
        block = outs[h].astype(jnp.bfloat16).reshape(requests, group_size, lane_count)
        for r in range(requests):
            out_ref[pl.ds((r * heads + h) * group_size, group_size), :] = block[r]
        all_rows += column_to_rows(levels[h], same)
    stats = jnp.concatenate(all_rows, axis=0)
    pieces = [piece.astype(jnp.float32) for piece in split_stat(stats)]
    spare = stat_rows(rows) - stat_pieces * stats.shape[0]
    if spare:
        pieces.append(jnp.zeros((spare, lane_count), jnp.float32))
    out_ref[pl.ds(rows, stat_rows(rows)), :] = jnp.concatenate(pieces, axis=0).astype(jnp.bfloat16)


def load_packed(in_ref, heads, requests, group_size, same):
    rows = requests * heads * group_size
    lines = rows // lane_count
    per_head = lines // heads
    stats = in_ref[pl.ds(rows, stat_rows(rows)), :].astype(jnp.float32)
    joined = stats[:lines]
    for piece in range(1, stat_pieces):
        joined = joined + stats[piece * lines : (piece + 1) * lines]
    outs, levels = [], []
    for h in range(heads):
        parts = [
            in_ref[pl.ds((r * heads + h) * group_size, group_size), :] for r in range(requests)
        ]
        outs.append(jnp.concatenate(parts, axis=0).astype(jnp.float32))
        lines_here = [joined[h * per_head + i : h * per_head + i + 1] for i in range(per_head)]
        levels.append(rows_to_column(lines_here, same))
    return outs, levels


def head_queries(query_ref, head, group_size):
    block = query_ref[:, head * group_size : (head + 1) * group_size, :]
    return block.reshape(block.shape[0] * group_size, block.shape[2])


def split_heads(source_ref, target_ref, wide_ref, shared, first, heads, base):
    tokens = source_ref.shape[0] // shared
    chunk = wide_ref.shape[0] // shared

    @pl.loop(0, tokens // chunk)
    def _(step):
        start = pl.multiple_of(step * chunk, chunk)
        rows = pl.multiple_of(step * (chunk * shared), chunk * shared)
        wide_ref[...] = source_ref[pl.ds(rows, chunk * shared), :].astype(jnp.float32)
        for h in range(heads):
            picked = wide_ref[pl.ds(first + h, chunk, stride=shared), :]
            target_ref[h, pl.ds(base + start, chunk), :] = picked.astype(target_ref.dtype)


def flat(cache):
    *lead, tokens, shared, width = cache.shape
    return cache.reshape(*lead, tokens * shared, width)


def packed_shape(query):
    requests, local_heads, width = query.shape
    rows = requests * local_heads
    return jax.ShapeDtypeStruct((rows + stat_rows(rows), width), query.dtype)


def root_pieces(query_ref, k_ref, v_ref, group_size):
    return lambda h: [(head_queries(query_ref, h, group_size), k_ref[h], v_ref[h], None)]


def first_kernel(
    scale, shared, pair_ref, query_ref, ko_ref, vo_ref, kp_ref, vp_ref, k_ref, v_ref, out_ref, wide_ref
):
    heads, both, _ = k_ref.shape
    first = pair_ref[0] * heads
    for base, keys, values in ((0, ko_ref, vo_ref), (both // 2, kp_ref, vp_ref)):
        split_heads(keys, k_ref, wide_ref, shared, first, heads, base)
        split_heads(values, v_ref, wide_ref, shared, first, heads, base)
    requests, local_heads, _ = query_ref.shape
    group_size = local_heads // heads
    pieces = root_pieces(query_ref, k_ref, v_ref, group_size)
    write_partials([(out_ref, pieces)], scale, heads, requests, group_size)


def first_block(pair_index, query, keys, values, other_keys, other_values, scale, heads):
    tokens, shared, width = keys.shape
    shape = jax.ShapeDtypeStruct((heads, 2 * tokens, width), keys.dtype)
    return pl.pallas_call(
        functools.partial(first_kernel, scale, shared),
        out_shape=(shape, shape, packed_shape(query)),
        in_specs=[smem_spec()] + [vmem_spec()] * 5,
        out_specs=(vmem_spec(),) * 3,
        scratch_shapes=[pltpu.VMEM((chunk_tokens * shared, width), jnp.float32)],
        compiler_params=kernel_params(),
        cost_estimate=light_cost(),
        name="first_block",
    )(pair_index, query, flat(keys), flat(values), flat(other_keys), flat(other_values))


def place_kernel(in_ref, out_ref):
    out_ref[0] = in_ref[0]


def place(pair_index):
    return pl.pallas_call(
        place_kernel,
        out_shape=jax.ShapeDtypeStruct(pair_index.shape, pair_index.dtype),
        in_specs=[smem_spec()],
        out_specs=smem_spec(),
        compiler_params=kernel_params(2**20),
        cost_estimate=pl.CostEstimate(flops=10**10, bytes_accessed=1, transcendentals=0),
        name="place",
    )(pair_index)


def root_kernel(scale, count, k_ref, v_ref, *refs):
    heads = k_ref.shape[0]
    requests, local_heads, _ = refs[0].shape
    group_size = local_heads // heads
    jobs = [
        (out_ref, root_pieces(query_ref, k_ref, v_ref, group_size))
        for query_ref, out_ref in zip(refs[:count], refs[count:])
    ]
    write_partials(jobs, scale, heads, requests, group_size)


def root_blocks(queries, keys, values, scale, after):
    return pl.pallas_call(
        ordered(functools.partial(root_kernel, scale, len(queries)), after),
        out_shape=[packed_shape(query) for query in queries],
        in_specs=any_specs(after) + [vmem_spec()] * (2 + len(queries)),
        out_specs=[vmem_spec()] * len(queries),
        compiler_params=kernel_params(),
        cost_estimate=light_cost(),
        name="root_blocks",
    )(*after, keys, values, *queries)


def branch_pieces(query_ref, k_ref, v_ref, limit_ref, owner, heads, group_size):
    def pieces(h):
        query = head_queries(query_ref, h, group_size)
        at = owner * heads + h
        return [
            (query, k_ref[b, at], v_ref[b, at], limit_ref[b][:, :1]) for b in range(k_ref.shape[0])
        ]

    return pieces


def theirs_kernel(
    scale, heads, pair_ref, branch_ref, seen_ref, query_ref, bk_ref, bv_ref,
    out_ref, k_ref, v_ref, limit_ref, wide_ref,
):
    requests, local_heads, _ = query_ref.shape
    branches, shared, tokens, _ = k_ref.shape
    group_size = local_heads // heads
    for b in range(branches):
        split_heads(bk_ref.at[b], k_ref.at[b], wide_ref, shared, 0, shared, 0)
        split_heads(bv_ref.at[b], v_ref.at[b], wide_ref, shared, 0, shared, 0)
        for r in range(requests):
            here = branch_ref[r] % branches == b
            limit = jnp.where(here, seen_ref[r] - pair_ref[0] * tokens, 0)
            limit_ref[b, pl.ds(r * group_size, group_size), :] = jnp.full(
                (group_size, lane_count), limit, jnp.int32
            )
    owner = 1 - pair_ref[0]
    pieces = branch_pieces(query_ref, k_ref, v_ref, limit_ref, owner, heads, group_size)
    write_partials([(out_ref, pieces)], scale, heads, requests, group_size)


def mine_kernel(scale, heads, pair_ref, query_ref, k_ref, v_ref, limit_ref, *refs):
    *others, out_ref = refs
    requests, local_heads, _ = query_ref.shape
    group_size = local_heads // heads
    pieces = branch_pieces(query_ref, k_ref, v_ref, limit_ref, pair_ref[0], heads, group_size)
    write_partials([(out_ref, pieces)], scale, heads, requests, group_size, others)


def theirs_block(pair_index, branch, seen, query, keys, values, scale, heads, after):
    branches, tokens, shared, width = keys.shape
    requests, local_heads, _ = query.shape
    rows = requests * local_heads // heads
    held = jax.ShapeDtypeStruct((branches, shared, tokens, width), keys.dtype)
    limits = jax.ShapeDtypeStruct((branches, rows, lane_count), jnp.int32)
    return pl.pallas_call(
        ordered(functools.partial(theirs_kernel, scale, heads), after),
        out_shape=(packed_shape(query), held, held, limits),
        in_specs=any_specs(after) + [smem_spec()] * 3 + [vmem_spec()] * 3,
        out_specs=(vmem_spec(),) * 4,
        scratch_shapes=[pltpu.VMEM((chunk_tokens * shared, width), jnp.float32)],
        compiler_params=kernel_params(),
        cost_estimate=light_cost(),
        name="theirs_block",
    )(*after, pair_index, branch, seen, query, flat(keys), flat(values))


def mine_block(pair_index, query, keys, values, limits, others, scale, heads):
    return pl.pallas_call(
        functools.partial(mine_kernel, scale, heads),
        out_shape=packed_shape(query),
        in_specs=[smem_spec()] + [vmem_spec()] * (4 + len(others)),
        out_specs=vmem_spec(),
        compiler_params=kernel_params(),
        cost_estimate=light_cost(),
        name="mine_block",
    )(pair_index, query, keys, values, limits, *others)


def merge_kernel(last, heads, requests, group_size, *refs):
    ins, out_ref = refs[:-1], refs[-1]
    same = identity_mask()
    loaded = [load_packed(ref, heads, requests, group_size, same) for ref in ins]
    outs, levels = [], []
    for h in range(heads):
        out, level = combine([(o[h], l[h]) for o, l in loaded])
        outs.append(out)
        levels.append(level)
    if last:
        for h in range(heads):
            block = outs[h].astype(out_ref.dtype).reshape(requests, group_size, lane_count)
            out_ref[:, h * group_size : (h + 1) * group_size, :] = block
    else:
        store_packed(out_ref, heads, requests, group_size, outs, levels, same)


def merge(parts, last, heads, requests, group_size, after=()):
    if last:
        shape = (requests, heads * group_size, lane_count)
    else:
        shape = parts[0].shape
    return pl.pallas_call(
        ordered(functools.partial(merge_kernel, last, heads, requests, group_size), after),
        out_shape=jax.ShapeDtypeStruct(shape, parts[0].dtype),
        in_specs=any_specs(after) + [vmem_spec()] * len(parts),
        out_specs=vmem_spec(),
        compiler_params=kernel_params(),
        cost_estimate=light_cost(),
        name="merge_last" if last else "merge_some",
    )(*after, *parts)


def local(queries, root_keys, root_values, branch_keys, branch_values, request_branch, seen_tokens):
    requests, local_heads, width = queries.shape
    shared = root_keys.shape[1]
    blocks = lax.axis_size("blk")
    heads = shared // lax.axis_size("pair")
    group_size = local_heads // heads
    scale = math.log2(math.e) / math.sqrt(width)
    pair_index = place(lax.axis_index("pair").astype(jnp.int32).reshape(1))

    other_keys = exchange(root_keys, "pair", 1)
    other_values = exchange(root_values, "pair", 1)
    other_queries = exchange(queries, "pair", 1)
    direct = range(blocks - 1, 0, -2)
    arrived = {apart: exchange(queries, "blk", apart) for apart in direct}

    keys, values, own = first_block(
        pair_index, queries, root_keys, root_values, other_keys, other_values, scale, heads
    )
    groups = [(apart, apart ^ 1) for apart in direct if apart > 1]
    for far, near in groups:
        arrived[far], own = lax.optimization_barrier((arrived[far], own))
        arrived[near] = exchange(arrived[far], "blk", 1)
    order = sorted(arrived, key=lambda apart: (apart % 2 == 0, -apart))
    returned, previous = {}, ()
    for apart in order:
        previous = root_blocks([arrived[apart]], keys, values, scale, previous)
        returned[apart] = exchange(previous[0], "blk", apart)
    theirs, held_keys, held_values, limits = theirs_block(
        pair_index, request_branch, seen_tokens, other_queries, branch_keys, branch_values,
        scale, heads, previous,
    )
    from_partner = exchange(theirs, "pair", 1)
    early = [own] + [returned.pop(apart) for apart in order if apart > 2 and apart % 2]
    most = mine_block(pair_index, queries, held_keys, held_values, limits, early, scale, heads)
    most = merge([most, *returned.values()], False, heads, requests, group_size)
    return merge([most, from_partner], True, heads, requests, group_size)


def solution(mesh):
    in_specs = (
        P(("groups", "blk"), ("kv", "pair"), None),
        P(("groups", "blk", "pair"), "kv", None),
        P(("groups", "blk", "pair"), "kv", None),
        P(("groups", "blk"), "pair", "kv", None),
        P(("groups", "blk"), "pair", "kv", None),
        P(("groups", "blk")),
        P(("groups", "blk")),
    )
    out_specs = P(("groups", "blk"), ("kv", "pair"), None)
    return jax.shard_map(local, mesh=mesh, in_specs=in_specs, out_specs=out_specs, check_vma=False)
```

```python
import functools
import math

import jax
import jax.numpy as jnp
from jax import lax
from jax.experimental import pallas as pl
from jax.experimental.pallas import tpu as pltpu
from jax.sharding import PartitionSpec as P

masked_floor = -1e30
lowest_reference = -1e29
lane_count = 128
stat_pieces = 3
vmem_grant = 24 * 2**20
chunk_tokens = 256
least_total = 2.0**-60
most_total = 2.0**100


def vmem_spec():
    return pl.BlockSpec(memory_space=pltpu.VMEM)


def smem_spec():
    return pl.BlockSpec(memory_space=pltpu.SMEM)


def any_specs(operands):
    return [pl.BlockSpec(memory_space=pl.ANY)] * len(operands)


def ordered(kernel, after):
    return lambda *refs: kernel(*refs[len(after) :])


def light_cost():
    return pl.CostEstimate(flops=1, bytes_accessed=1, transcendentals=0)


def heavy_cost():
    return pl.CostEstimate(flops=10**10, bytes_accessed=1, transcendentals=0)


def kernel_params(grant=vmem_grant):
    return pltpu.CompilerParams(vmem_limit_bytes=grant)


def exchange(value, axis, apart):
    return lax.ppermute(value, axis, [(i, i ^ apart) for i in range(lax.axis_size(axis))])


def stat_rows(rows):
    return -(-stat_pieces * (rows // lane_count) // 16) * 16


def identity_mask():
    shape = (lane_count, lane_count)
    return lax.broadcasted_iota(jnp.int32, shape, 0) == lax.broadcasted_iota(jnp.int32, shape, 1)


def column_to_rows(column, same):
    pieces = []
    for start in range(0, column.shape[0], lane_count):
        wide = jnp.broadcast_to(column[start : start + lane_count], (lane_count, lane_count))
        pieces.append(jnp.sum(jnp.where(same, wide, 0.0), axis=0, keepdims=True))
    return pieces


def rows_to_column(pieces, same):
    columns = []
    for piece in pieces:
        wide = jnp.broadcast_to(piece, (lane_count, lane_count))
        columns.append(jnp.sum(jnp.where(same, wide, 0.0), axis=1, keepdims=True))
    return jnp.concatenate(columns, axis=0)


def split_stat(value):
    pieces = []
    for _ in range(stat_pieces):
        piece = value.astype(jnp.bfloat16)
        pieces.append(piece)
        value = value - piece.astype(jnp.float32)
    return pieces


def evaluate(pieces, scale, exact):
    state = None
    hidden = None
    for query, keys, values, limits in pieces:
        scores = lax.dot_general(
            query, keys, (((1,), (1,)), ((), ())), preferred_element_type=jnp.float32
        )
        seen = None
        if limits is not None:
            each = scores.shape[1] // len(limits)
            ends = [limit for limit in limits for _ in range(each // lane_count)]
            seen = lax.broadcasted_iota(jnp.int32, scores.shape, 1) < jnp.concatenate(ends, axis=1)
            counts = [limit - b * each for b, limit in enumerate(limits)]
            most = functools.reduce(jnp.maximum, counts)
            hidden = jnp.where(most > 0, 0.0, 1.0)[:, :1]
        if exact:
            if seen is not None:
                scores = jnp.where(seen, scores, masked_floor)
            largest = jnp.max(scores, axis=1, keepdims=True)
            if seen is not None:
                largest = jnp.maximum(largest, lowest_reference)
            weights = jnp.exp2((scores - largest) * scale)
            largest = largest * scale
        else:
            weights = jnp.exp2(scores * scale)
            if seen is not None:
                weights = jnp.where(seen, weights, 0.0)
        totals = jnp.sum(weights, axis=1, keepdims=True)
        sums = jnp.dot(weights.astype(jnp.bfloat16), values, preferred_element_type=jnp.float32)
        if state is None:
            state = (sums, totals, largest if exact else None)
        elif exact:
            top = jnp.maximum(state[2], largest)
            one, two = jnp.exp2(state[2] - top), jnp.exp2(largest - top)
            state = (state[0] * one + sums * two, state[1] * one + totals * two, top)
        else:
            state = (state[0] + sums, state[1] + totals, None)
    sums, totals, largest = state
    sound = jnp.where((totals > least_total) & (totals < most_total), 1.0, 0.0)
    if hidden is not None:
        sound = jnp.maximum(sound, hidden)
        totals = totals + hidden
    level = jnp.log2(totals)
    if exact:
        level = level + largest
    if hidden is not None:
        level = level + hidden * masked_floor
    return sums * (1.0 / totals), level, sound


def combine(parts):
    top = parts[0][1]
    for _, level in parts[1:]:
        top = jnp.maximum(top, level)
    sums = totals = 0.0
    for out, level in parts:
        weight = jnp.exp2(level - top)
        sums = sums + out * weight
        totals = totals + weight
    return sums * (1.0 / totals), top + jnp.log2(totals)


def write_partials(jobs, scale, heads, requests, group_size, others=()):
    same = identity_mask()

    loaded = [load_packed(ref, heads, requests, group_size, same) for ref in others]

    def run(exact):
        least = 1.0
        for out_ref, pieces_of in jobs:
            outs, levels = [], []
            for h in range(heads):
                out, level, sound = evaluate(pieces_of(h), scale, exact)
                if others:
                    added = [(o[h], l[h]) for o, l in loaded]
                    out, level = combine([(out, level), *added])
                outs.append(out)
                levels.append(level)
                least = jnp.minimum(least, sound)
            store_packed(out_ref, heads, requests, group_size, outs, levels, same)
        return jnp.min(least)

    least = run(False)

    @pl.when(least < 0.5)
    def _():
        run(True)


def store_packed(out_ref, heads, requests, group_size, outs, levels, same):
    rows = requests * heads * group_size
    per_head = requests * group_size
    all_rows = []
    for h in range(heads):
        block = outs[h].astype(jnp.bfloat16).reshape(requests, group_size, lane_count)
        for r in range(requests):
            out_ref[pl.ds((r * heads + h) * group_size, group_size), :] = block[r]
        all_rows += column_to_rows(levels[h], same)
    stats = jnp.concatenate(all_rows, axis=0)
    pieces = [piece.astype(jnp.float32) for piece in split_stat(stats)]
    spare = stat_rows(rows) - stat_pieces * stats.shape[0]
    if spare:
        pieces.append(jnp.zeros((spare, lane_count), jnp.float32))
    out_ref[pl.ds(rows, stat_rows(rows)), :] = jnp.concatenate(pieces, axis=0).astype(jnp.bfloat16)


def load_packed(in_ref, heads, requests, group_size, same):
    rows = requests * heads * group_size
    lines = rows // lane_count
    per_head = lines // heads
    stats = in_ref[pl.ds(rows, stat_rows(rows)), :].astype(jnp.float32)
    joined = stats[:lines]
    for piece in range(1, stat_pieces):
        joined = joined + stats[piece * lines : (piece + 1) * lines]
    outs, levels = [], []
    for h in range(heads):
        parts = [
            in_ref[pl.ds((r * heads + h) * group_size, group_size), :] for r in range(requests)
        ]
        outs.append(jnp.concatenate(parts, axis=0).astype(jnp.float32))
        lines_here = [joined[h * per_head + i : h * per_head + i + 1] for i in range(per_head)]
        levels.append(rows_to_column(lines_here, same))
    return outs, levels


def head_queries(query_ref, head, group_size):
    block = query_ref[:, head * group_size : (head + 1) * group_size, :]
    return block.reshape(block.shape[0] * group_size, block.shape[2])


def split_heads(source_ref, target_ref, wide_ref, shared, first, heads, base):
    tokens = source_ref.shape[0] // shared
    chunk = wide_ref.shape[0] // shared

    @pl.loop(0, tokens // chunk)
    def _(step):
        start = pl.multiple_of(step * chunk, chunk)
        rows = pl.multiple_of(step * (chunk * shared), chunk * shared)
        wide_ref[...] = source_ref[pl.ds(rows, chunk * shared), :].astype(jnp.float32)
        for h in range(heads):
            picked = wide_ref[pl.ds(first + h, chunk, stride=shared), :]
            target_ref[h, pl.ds(base + start, chunk), :] = picked.astype(target_ref.dtype)


def flat(cache):
    *lead, tokens, shared, width = cache.shape
    return cache.reshape(*lead, tokens * shared, width)


def packed_shape(query):
    requests, local_heads, width = query.shape
    rows = requests * local_heads
    return jax.ShapeDtypeStruct((rows + stat_rows(rows), width), query.dtype)


def root_pieces(query_ref, k_ref, v_ref, group_size):
    return lambda h: [(head_queries(query_ref, h, group_size), k_ref[h], v_ref[h], None)]


def first_kernel(
    scale, shared, query_ref, ko_ref, vo_ref, kp_ref, vp_ref, k_ref, v_ref, out_ref, wide_ref
):
    heads, both, _ = k_ref.shape
    first = lax.axis_index("pair") * heads
    for base, keys, values in ((0, ko_ref, vo_ref), (both // 2, kp_ref, vp_ref)):
        split_heads(keys, k_ref, wide_ref, shared, first, heads, base)
        split_heads(values, v_ref, wide_ref, shared, first, heads, base)
    requests, local_heads, _ = query_ref.shape
    group_size = local_heads // heads
    pieces = root_pieces(query_ref, k_ref, v_ref, group_size)
    write_partials([(out_ref, pieces)], scale, heads, requests, group_size)


def first_block(query, keys, values, other_keys, other_values, scale, heads, after):
    tokens, shared, width = keys.shape
    shape = jax.ShapeDtypeStruct((heads, 2 * tokens, width), keys.dtype)
    return pl.pallas_call(
        ordered(functools.partial(first_kernel, scale, shared), after),
        out_shape=(shape, shape, packed_shape(query)),
        in_specs=any_specs(after) + [vmem_spec()] * 5,
        out_specs=(vmem_spec(),) * 3,
        scratch_shapes=[pltpu.VMEM((chunk_tokens * shared, width), jnp.float32)],
        compiler_params=kernel_params(),
        cost_estimate=light_cost(),
        name="first_block",
    )(*after, query, flat(keys), flat(values), flat(other_keys), flat(other_values))


def limits_kernel(tokens, group_size, branch_ref, seen_ref, limit_ref):
    branches = limit_ref.shape[0]
    before = lax.axis_index("pair") * tokens
    for b in range(branches):
        for r in range(branch_ref.shape[0]):
            here = branch_ref[r] % branches == b
            count = jnp.clip(seen_ref[r] - before, 0, tokens)
            limit = b * tokens + jnp.where(here, count, 0)
            limit_ref[b, pl.ds(r * group_size, group_size), :] = jnp.full(
                (group_size, lane_count), limit, jnp.int32
            )


def limits_block(branch, seen, branches, tokens, group_size):
    shape = (branches, branch.shape[0] * group_size, lane_count)
    return pl.pallas_call(
        functools.partial(limits_kernel, tokens, group_size),
        out_shape=jax.ShapeDtypeStruct(shape, jnp.int32),
        in_specs=[smem_spec()] * 2,
        out_specs=vmem_spec(),
        compiler_params=kernel_params(2**20),
        cost_estimate=heavy_cost(),
        name="limits_block",
    )(branch, seen)


def root_kernel(scale, count, k_ref, v_ref, *refs):
    heads = k_ref.shape[0]
    requests, local_heads, _ = refs[0].shape
    group_size = local_heads // heads
    jobs = [
        (out_ref, root_pieces(query_ref, k_ref, v_ref, group_size))
        for query_ref, out_ref in zip(refs[:count], refs[count:])
    ]
    write_partials(jobs, scale, heads, requests, group_size)


def root_blocks(queries, keys, values, scale, after):
    return pl.pallas_call(
        ordered(functools.partial(root_kernel, scale, len(queries)), after),
        out_shape=[packed_shape(query) for query in queries],
        in_specs=any_specs(after) + [vmem_spec()] * (2 + len(queries)),
        out_specs=[vmem_spec()] * len(queries),
        compiler_params=kernel_params(),
        cost_estimate=light_cost(),
        name="root_blocks",
    )(*after, keys, values, *queries)


def branch_pieces(query_ref, k_ref, v_ref, limit_ref, owner, heads, group_size):
    def pieces(h):
        at = owner * heads + h
        limits = [limit_ref[b] for b in range(limit_ref.shape[0])]
        return [(head_queries(query_ref, h, group_size), k_ref[at], v_ref[at], limits)]

    return pieces


def theirs_kernel(
    scale, heads, limit_ref, query_ref, bk_ref, bv_ref, out_ref, k_ref, v_ref, wide_ref
):
    requests, local_heads, _ = query_ref.shape
    shared, slots, _ = k_ref.shape
    branches = bk_ref.shape[0]
    group_size = local_heads // heads
    for b in range(branches):
        base = b * (slots // branches)
        split_heads(bk_ref.at[b], k_ref, wide_ref, shared, 0, shared, base)
        split_heads(bv_ref.at[b], v_ref, wide_ref, shared, 0, shared, base)
    owner = 1 - lax.axis_index("pair")
    pieces = branch_pieces(query_ref, k_ref, v_ref, limit_ref, owner, heads, group_size)
    write_partials([(out_ref, pieces)], scale, heads, requests, group_size)


def mine_kernel(scale, heads, limit_ref, query_ref, k_ref, v_ref, *refs):
    *others, out_ref = refs
    requests, local_heads, _ = query_ref.shape
    group_size = local_heads // heads
    owner = lax.axis_index("pair")
    pieces = branch_pieces(query_ref, k_ref, v_ref, limit_ref, owner, heads, group_size)
    write_partials([(out_ref, pieces)], scale, heads, requests, group_size, others)


def theirs_block(limits, query, keys, values, scale, heads, after):
    branches, tokens, shared, width = keys.shape
    held = jax.ShapeDtypeStruct((shared, branches * tokens, width), keys.dtype)
    return pl.pallas_call(
        ordered(functools.partial(theirs_kernel, scale, heads), after),
        out_shape=(packed_shape(query), held, held),
        in_specs=any_specs(after) + [vmem_spec()] * 4,
        out_specs=(vmem_spec(),) * 3,
        scratch_shapes=[pltpu.VMEM((chunk_tokens * shared, width), jnp.float32)],
        compiler_params=kernel_params(),
        cost_estimate=light_cost(),
        name="theirs_block",
    )(*after, limits, query, flat(keys), flat(values))


def mine_block(limits, query, keys, values, others, scale, heads):
    return pl.pallas_call(
        functools.partial(mine_kernel, scale, heads),
        out_shape=packed_shape(query),
        in_specs=[vmem_spec()] * (4 + len(others)),
        out_specs=vmem_spec(),
        compiler_params=kernel_params(),
        cost_estimate=heavy_cost(),
        name="mine_block",
    )(limits, query, keys, values, *others)


def merge_kernel(last, heads, requests, group_size, *refs):
    ins, out_ref = refs[:-1], refs[-1]
    same = identity_mask()
    loaded = [load_packed(ref, heads, requests, group_size, same) for ref in ins]
    outs, levels = [], []
    for h in range(heads):
        out, level = combine([(o[h], l[h]) for o, l in loaded])
        outs.append(out)
        levels.append(level)
    if last:
        for h in range(heads):
            block = outs[h].astype(out_ref.dtype).reshape(requests, group_size, lane_count)
            out_ref[:, h * group_size : (h + 1) * group_size, :] = block
    else:
        store_packed(out_ref, heads, requests, group_size, outs, levels, same)


def merge(parts, last, heads, requests, group_size, after=()):
    if last:
        shape = (requests, heads * group_size, lane_count)
    else:
        shape = parts[0].shape
    return pl.pallas_call(
        ordered(functools.partial(merge_kernel, last, heads, requests, group_size), after),
        out_shape=jax.ShapeDtypeStruct(shape, parts[0].dtype),
        in_specs=any_specs(after) + [vmem_spec()] * len(parts),
        out_specs=vmem_spec(),
        compiler_params=kernel_params(),
        cost_estimate=light_cost(),
        name="merge_last" if last else "merge_some",
    )(*after, *parts)


def local(queries, root_keys, root_values, branch_keys, branch_values, request_branch, seen_tokens):
    requests, local_heads, width = queries.shape
    shared = root_keys.shape[1]
    blocks = lax.axis_size("blk")
    heads = shared // lax.axis_size("pair")
    group_size = local_heads // heads
    scale = math.log2(math.e) / math.sqrt(width)
    branches, tokens, _, _ = branch_keys.shape
    limits = limits_block(request_branch, seen_tokens, branches, tokens, group_size)

    other_keys = exchange(root_keys, "pair", 1)
    other_values = exchange(root_values, "pair", 1)
    other_queries = exchange(queries, "pair", 1)
    direct = range(blocks - 1, 0, -2)
    arrived = {apart: exchange(queries, "blk", apart) for apart in direct}

    keys, values, own = first_block(
        queries, root_keys, root_values, other_keys, other_values, scale, heads, (limits,)
    )
    groups = [(apart, apart ^ 1) for apart in direct if apart > 1]
    for far, near in groups:
        arrived[far], own = lax.optimization_barrier((arrived[far], own))
        arrived[near] = exchange(arrived[far], "blk", 1)
    order = sorted(arrived, key=lambda apart: (apart % 2 == 0, -apart))
    returned, previous = {}, ()
    for apart in order:
        previous = root_blocks([arrived[apart]], keys, values, scale, previous)
        returned[apart] = exchange(previous[0], "blk", apart)
    theirs, held_keys, held_values = theirs_block(
        limits, other_queries, branch_keys, branch_values, scale, heads, previous
    )
    from_partner = exchange(theirs, "pair", 1)
    mine = mine_block(limits, queries, held_keys, held_values, [own], scale, heads)
    last = returned.pop(order[-1])
    most = merge([mine, from_partner, *returned.values()], False, heads, requests, group_size)
    return merge([most, last], True, heads, requests, group_size)


def solution(mesh):
    in_specs = (
        P(("groups", "blk"), ("kv", "pair"), None),
        P(("groups", "blk", "pair"), "kv", None),
        P(("groups", "blk", "pair"), "kv", None),
        P(("groups", "blk"), "pair", "kv", None),
        P(("groups", "blk"), "pair", "kv", None),
        P(("groups", "blk")),
        P(("groups", "blk")),
    )
    out_specs = P(("groups", "blk"), ("kv", "pair"), None)
    return jax.shard_map(local, mesh=mesh, in_specs=in_specs, out_specs=out_specs, check_vma=False)
```

```python
import functools
import math

import jax
import jax.numpy as jnp
from jax import lax
from jax.experimental import pallas as pl
from jax.experimental.pallas import tpu as pltpu
from jax.sharding import PartitionSpec as P

masked_floor = -1e30
lowest_reference = -1e29
lane_count = 128
stat_pieces = 3
vmem_grant = 24 * 2**20
chunk_tokens = 256
least_total = 2.0**-60
most_total = 2.0**100


def vmem_spec():
    return pl.BlockSpec(memory_space=pltpu.VMEM)


def smem_spec():
    return pl.BlockSpec(memory_space=pltpu.SMEM)


def any_specs(operands):
    return [pl.BlockSpec(memory_space=pl.ANY)] * len(operands)


def ordered(kernel, after):
    return lambda *refs: kernel(*refs[len(after) :])


def light_cost():
    return pl.CostEstimate(flops=1, bytes_accessed=1, transcendentals=0)


def heavy_cost():
    return pl.CostEstimate(flops=10**10, bytes_accessed=1, transcendentals=0)


def kernel_params(grant=vmem_grant):
    return pltpu.CompilerParams(vmem_limit_bytes=grant)


def exchange(value, axis, apart):
    return lax.ppermute(value, axis, [(i, i ^ apart) for i in range(lax.axis_size(axis))])


def stat_rows(rows):
    return -(-stat_pieces * (rows // lane_count) // 16) * 16


def identity_mask():
    shape = (lane_count, lane_count)
    return lax.broadcasted_iota(jnp.int32, shape, 0) == lax.broadcasted_iota(jnp.int32, shape, 1)


def column_to_rows(column, same):
    pieces = []
    for start in range(0, column.shape[0], lane_count):
        wide = jnp.broadcast_to(column[start : start + lane_count], (lane_count, lane_count))
        pieces.append(jnp.sum(jnp.where(same, wide, 0.0), axis=0, keepdims=True))
    return pieces


def rows_to_column(pieces, same):
    columns = []
    for piece in pieces:
        wide = jnp.broadcast_to(piece, (lane_count, lane_count))
        columns.append(jnp.sum(jnp.where(same, wide, 0.0), axis=1, keepdims=True))
    return jnp.concatenate(columns, axis=0)


def split_stat(value):
    pieces = []
    for _ in range(stat_pieces):
        piece = value.astype(jnp.bfloat16)
        pieces.append(piece)
        value = value - piece.astype(jnp.float32)
    return pieces


def evaluate(pieces, scale, exact):
    state = None
    hidden = None
    for query, keys, values, limits in pieces:
        scores = lax.dot_general(
            query, keys, (((1,), (1,)), ((), ())), preferred_element_type=jnp.float32
        )
        seen = None
        if limits is not None:
            each = scores.shape[1] // len(limits)
            ends = [limit for limit in limits for _ in range(each // lane_count)]
            seen = lax.broadcasted_iota(jnp.int32, scores.shape, 1) < jnp.concatenate(ends, axis=1)
            counts = [limit - b * each for b, limit in enumerate(limits)]
            most = functools.reduce(jnp.maximum, counts)
            hidden = jnp.where(most > 0, 0.0, 1.0)[:, :1]
        if exact:
            if seen is not None:
                scores = jnp.where(seen, scores, masked_floor)
            largest = jnp.max(scores, axis=1, keepdims=True)
            if seen is not None:
                largest = jnp.maximum(largest, lowest_reference)
            weights = jnp.exp2((scores - largest) * scale)
            largest = largest * scale
        else:
            weights = jnp.exp2(scores * scale)
            if seen is not None:
                weights = jnp.where(seen, weights, 0.0)
        totals = jnp.sum(weights, axis=1, keepdims=True)
        sums = jnp.dot(weights.astype(jnp.bfloat16), values, preferred_element_type=jnp.float32)
        if state is None:
            state = (sums, totals, largest if exact else None)
        elif exact:
            top = jnp.maximum(state[2], largest)
            one, two = jnp.exp2(state[2] - top), jnp.exp2(largest - top)
            state = (state[0] * one + sums * two, state[1] * one + totals * two, top)
        else:
            state = (state[0] + sums, state[1] + totals, None)
    sums, totals, largest = state
    sound = jnp.where((totals > least_total) & (totals < most_total), 1.0, 0.0)
    if hidden is not None:
        sound = jnp.maximum(sound, hidden)
        totals = totals + hidden
    level = jnp.log2(totals)
    if exact:
        level = level + largest
    if hidden is not None:
        level = level + hidden * masked_floor
    return sums * (1.0 / totals), level, sound


def combine(parts):
    top = parts[0][1]
    for _, level in parts[1:]:
        top = jnp.maximum(top, level)
    sums = totals = 0.0
    for out, level in parts:
        weight = jnp.exp2(level - top)
        sums = sums + out * weight
        totals = totals + weight
    return sums * (1.0 / totals), top + jnp.log2(totals)


def write_partials(jobs, scale, heads, requests, group_size, others=()):
    same = identity_mask()

    loaded = [load_packed(ref, heads, requests, group_size, same) for ref in others]

    def run(exact):
        least = 1.0
        for out_ref, pieces_of in jobs:
            outs, levels = [], []
            for h in range(heads):
                out, level, sound = evaluate(pieces_of(h), scale, exact)
                if others:
                    added = [(o[h], l[h]) for o, l in loaded]
                    out, level = combine([(out, level), *added])
                outs.append(out)
                levels.append(level)
                least = jnp.minimum(least, sound)
            store_packed(out_ref, heads, requests, group_size, outs, levels, same)
        return jnp.min(least)

    least = run(False)

    @pl.when(least < 0.5)
    def _():
        run(True)


def store_packed(out_ref, heads, requests, group_size, outs, levels, same):
    rows = requests * heads * group_size
    per_head = requests * group_size
    all_rows = []
    for h in range(heads):
        block = outs[h].astype(jnp.bfloat16).reshape(requests, group_size, lane_count)
        for r in range(requests):
            out_ref[pl.ds((r * heads + h) * group_size, group_size), :] = block[r]
        all_rows += column_to_rows(levels[h], same)
    stats = jnp.concatenate(all_rows, axis=0)
    pieces = [piece.astype(jnp.float32) for piece in split_stat(stats)]
    spare = stat_rows(rows) - stat_pieces * stats.shape[0]
    if spare:
        pieces.append(jnp.zeros((spare, lane_count), jnp.float32))
    out_ref[pl.ds(rows, stat_rows(rows)), :] = jnp.concatenate(pieces, axis=0).astype(jnp.bfloat16)


def load_packed(in_ref, heads, requests, group_size, same):
    rows = requests * heads * group_size
    lines = rows // lane_count
    per_head = lines // heads
    stats = in_ref[pl.ds(rows, stat_rows(rows)), :].astype(jnp.float32)
    joined = stats[:lines]
    for piece in range(1, stat_pieces):
        joined = joined + stats[piece * lines : (piece + 1) * lines]
    outs, levels = [], []
    for h in range(heads):
        parts = [
            in_ref[pl.ds((r * heads + h) * group_size, group_size), :] for r in range(requests)
        ]
        outs.append(jnp.concatenate(parts, axis=0).astype(jnp.float32))
        lines_here = [joined[h * per_head + i : h * per_head + i + 1] for i in range(per_head)]
        levels.append(rows_to_column(lines_here, same))
    return outs, levels


def head_queries(query_ref, head, group_size):
    block = query_ref[:, head * group_size : (head + 1) * group_size, :]
    return block.reshape(block.shape[0] * group_size, block.shape[2])


def split_heads(source_ref, target_ref, wide_ref, shared, first, heads, base):
    tokens = source_ref.shape[0] // shared
    chunk = wide_ref.shape[0] // shared

    @pl.loop(0, tokens // chunk)
    def _(step):
        start = pl.multiple_of(step * chunk, chunk)
        rows = pl.multiple_of(step * (chunk * shared), chunk * shared)
        wide_ref[...] = source_ref[pl.ds(rows, chunk * shared), :].astype(jnp.float32)
        for h in range(heads):
            picked = wide_ref[pl.ds(first + h, chunk, stride=shared), :]
            target_ref[h, pl.ds(base + start, chunk), :] = picked.astype(target_ref.dtype)


def flat(cache):
    *lead, tokens, shared, width = cache.shape
    return cache.reshape(*lead, tokens * shared, width)


def packed_shape(query):
    requests, local_heads, width = query.shape
    rows = requests * local_heads
    return jax.ShapeDtypeStruct((rows + stat_rows(rows), width), query.dtype)


def root_pieces(query_ref, k_ref, v_ref, group_size):
    return lambda h: [(head_queries(query_ref, h, group_size), k_ref[h], v_ref[h], None)]


def first_kernel(
    scale, shared, query_ref, ko_ref, vo_ref, kp_ref, vp_ref, k_ref, v_ref, out_ref, wide_ref
):
    heads, both, _ = k_ref.shape
    first = lax.axis_index("pair") * heads
    for base, keys, values in ((0, ko_ref, vo_ref), (both // 2, kp_ref, vp_ref)):
        split_heads(keys, k_ref, wide_ref, shared, first, heads, base)
        split_heads(values, v_ref, wide_ref, shared, first, heads, base)
    requests, local_heads, _ = query_ref.shape
    group_size = local_heads // heads
    pieces = root_pieces(query_ref, k_ref, v_ref, group_size)
    write_partials([(out_ref, pieces)], scale, heads, requests, group_size)


def first_block(query, keys, values, other_keys, other_values, scale, heads, after):
    tokens, shared, width = keys.shape
    shape = jax.ShapeDtypeStruct((heads, 2 * tokens, width), keys.dtype)
    return pl.pallas_call(
        ordered(functools.partial(first_kernel, scale, shared), after),
        out_shape=(shape, shape, packed_shape(query)),
        in_specs=any_specs(after) + [vmem_spec()] * 5,
        out_specs=(vmem_spec(),) * 3,
        scratch_shapes=[pltpu.VMEM((chunk_tokens * shared, width), jnp.float32)],
        compiler_params=kernel_params(),
        cost_estimate=light_cost(),
        name="first_block",
    )(*after, query, flat(keys), flat(values), flat(other_keys), flat(other_values))


def limits_kernel(tokens, group_size, branch_ref, seen_ref, limit_ref):
    branches = limit_ref.shape[0]
    before = lax.axis_index("pair") * tokens
    for b in range(branches):
        for r in range(branch_ref.shape[0]):
            here = branch_ref[r] % branches == b
            count = jnp.clip(seen_ref[r] - before, 0, tokens)
            limit = b * tokens + jnp.where(here, count, 0)
            limit_ref[b, pl.ds(r * group_size, group_size), :] = jnp.full(
                (group_size, lane_count), limit, jnp.int32
            )


def limits_block(branch, seen, branches, tokens, group_size, after):
    shape = (branches, branch.shape[0] * group_size, lane_count)
    return pl.pallas_call(
        ordered(functools.partial(limits_kernel, tokens, group_size), after),
        out_shape=jax.ShapeDtypeStruct(shape, jnp.int32),
        in_specs=any_specs(after) + [smem_spec()] * 2,
        out_specs=vmem_spec(),
        compiler_params=kernel_params(2**20),
        cost_estimate=light_cost(),
        name="limits_block",
    )(*after, branch, seen)


def mark_kernel(out_ref):
    out_ref[...] = jnp.zeros_like(out_ref)


def mark():
    return pl.pallas_call(
        mark_kernel,
        out_shape=jax.ShapeDtypeStruct((8, lane_count), jnp.float32),
        out_specs=vmem_spec(),
        compiler_params=kernel_params(2**20),
        cost_estimate=heavy_cost(),
        name="mark",
    )()


def root_kernel(scale, count, k_ref, v_ref, *refs):
    heads = k_ref.shape[0]
    requests, local_heads, _ = refs[0].shape
    group_size = local_heads // heads
    jobs = [
        (out_ref, root_pieces(query_ref, k_ref, v_ref, group_size))
        for query_ref, out_ref in zip(refs[:count], refs[count:])
    ]
    write_partials(jobs, scale, heads, requests, group_size)


def root_blocks(queries, keys, values, scale, after):
    return pl.pallas_call(
        ordered(functools.partial(root_kernel, scale, len(queries)), after),
        out_shape=[packed_shape(query) for query in queries],
        in_specs=any_specs(after) + [vmem_spec()] * (2 + len(queries)),
        out_specs=[vmem_spec()] * len(queries),
        compiler_params=kernel_params(),
        cost_estimate=light_cost(),
        name="root_blocks",
    )(*after, keys, values, *queries)


def branch_pieces(query_ref, k_ref, v_ref, limit_ref, owner, heads, group_size):
    def pieces(h):
        at = owner * heads + h
        limits = [limit_ref[b] for b in range(limit_ref.shape[0])]
        return [(head_queries(query_ref, h, group_size), k_ref[at], v_ref[at], limits)]

    return pieces


def theirs_kernel(
    scale, heads, limit_ref, query_ref, bk_ref, bv_ref, out_ref, k_ref, v_ref, wide_ref
):
    requests, local_heads, _ = query_ref.shape
    shared, slots, _ = k_ref.shape
    branches = bk_ref.shape[0]
    group_size = local_heads // heads
    for b in range(branches):
        base = b * (slots // branches)
        split_heads(bk_ref.at[b], k_ref, wide_ref, shared, 0, shared, base)
        split_heads(bv_ref.at[b], v_ref, wide_ref, shared, 0, shared, base)
    owner = 1 - lax.axis_index("pair")
    pieces = branch_pieces(query_ref, k_ref, v_ref, limit_ref, owner, heads, group_size)
    write_partials([(out_ref, pieces)], scale, heads, requests, group_size)


def mine_kernel(scale, heads, limit_ref, query_ref, k_ref, v_ref, *refs):
    *others, out_ref = refs
    requests, local_heads, _ = query_ref.shape
    group_size = local_heads // heads
    owner = lax.axis_index("pair")
    pieces = branch_pieces(query_ref, k_ref, v_ref, limit_ref, owner, heads, group_size)
    write_partials([(out_ref, pieces)], scale, heads, requests, group_size, others)


def theirs_block(limits, query, keys, values, scale, heads, after):
    branches, tokens, shared, width = keys.shape
    held = jax.ShapeDtypeStruct((shared, branches * tokens, width), keys.dtype)
    return pl.pallas_call(
        ordered(functools.partial(theirs_kernel, scale, heads), after),
        out_shape=(packed_shape(query), held, held),
        in_specs=any_specs(after) + [vmem_spec()] * 4,
        out_specs=(vmem_spec(),) * 3,
        scratch_shapes=[pltpu.VMEM((chunk_tokens * shared, width), jnp.float32)],
        compiler_params=kernel_params(),
        cost_estimate=light_cost(),
        name="theirs_block",
    )(*after, limits, query, flat(keys), flat(values))


def mine_block(limits, query, keys, values, others, scale, heads):
    return pl.pallas_call(
        functools.partial(mine_kernel, scale, heads),
        out_shape=packed_shape(query),
        in_specs=[vmem_spec()] * (4 + len(others)),
        out_specs=vmem_spec(),
        compiler_params=kernel_params(),
        cost_estimate=heavy_cost(),
        name="mine_block",
    )(limits, query, keys, values, *others)


def gather_kernel(requests, group_size, *refs):
    *ins, sums_ref, level_ref = refs
    heads = sums_ref.shape[0]
    same = identity_mask()
    loaded = [load_packed(ref, heads, requests, group_size, same) for ref in ins]
    for h in range(heads):
        out, level = combine([(o[h], l[h]) for o, l in loaded])
        sums_ref[h] = out
        level_ref[h] = jnp.broadcast_to(level, out.shape)


def gather_partials(parts, heads, requests, group_size):
    shape = jax.ShapeDtypeStruct((heads, requests * group_size, lane_count), jnp.float32)
    return pl.pallas_call(
        functools.partial(gather_kernel, requests, group_size),
        out_shape=(shape, shape),
        in_specs=[vmem_spec()] * len(parts),
        out_specs=(vmem_spec(), vmem_spec()),
        compiler_params=kernel_params(),
        cost_estimate=light_cost(),
        name="gather_partials",
    )(*parts)


def last_kernel(requests, group_size, sums_ref, level_ref, back_ref, out_ref):
    heads = sums_ref.shape[0]
    outs, levels = load_packed(back_ref, heads, requests, group_size, identity_mask())
    for h in range(heads):
        parts = [(sums_ref[h], level_ref[h]), (outs[h], levels[h])]
        out, _ = combine(parts)
        block = out.astype(out_ref.dtype).reshape(requests, group_size, lane_count)
        out_ref[:, h * group_size : (h + 1) * group_size, :] = block


def merge_last(sums, levels, back, requests, group_size):
    shape = (requests, sums.shape[0] * group_size, lane_count)
    return pl.pallas_call(
        functools.partial(last_kernel, requests, group_size),
        out_shape=jax.ShapeDtypeStruct(shape, back.dtype),
        in_specs=[vmem_spec()] * 3,
        out_specs=vmem_spec(),
        compiler_params=kernel_params(),
        cost_estimate=light_cost(),
        name="merge_last",
    )(sums, levels, back)


def local(queries, root_keys, root_values, branch_keys, branch_values, request_branch, seen_tokens):
    requests, local_heads, width = queries.shape
    shared = root_keys.shape[1]
    blocks = lax.axis_size("blk")
    heads = shared // lax.axis_size("pair")
    group_size = local_heads // heads
    scale = math.log2(math.e) / math.sqrt(width)

    other_keys = exchange(root_keys, "pair", 1)
    other_values = exchange(root_values, "pair", 1)
    other_queries = exchange(queries, "pair", 1)
    direct = range(blocks - 1, 0, -2)
    arrived = {apart: exchange(queries, "blk", apart) for apart in direct}

    keys, values, own = first_block(
        queries, root_keys, root_values, other_keys, other_values, scale, heads, (mark(),)
    )
    groups = [(apart, apart ^ 1) for apart in direct if apart > 1]
    for far, near in groups:
        arrived[far], own = lax.optimization_barrier((arrived[far], own))
        arrived[near] = exchange(arrived[far], "blk", 1)
    order = sorted(arrived, key=lambda apart: (apart % 2 == 0, -apart))
    returned, previous = {}, ()
    for apart in order:
        previous = root_blocks([arrived[apart]], keys, values, scale, previous)
        returned[apart] = exchange(previous[0], "blk", apart)
    branches, tokens, _, _ = branch_keys.shape
    limits = limits_block(
        request_branch, seen_tokens, branches, tokens, group_size, previous
    )
    theirs, held_keys, held_values = theirs_block(
        limits, other_queries, branch_keys, branch_values, scale, heads, previous
    )
    from_partner = exchange(theirs, "pair", 1)
    mine = mine_block(limits, queries, held_keys, held_values, [own], scale, heads)
    last = returned.pop(order[-1])
    parts = [mine, from_partner, *returned.values()]
    sums, levels = gather_partials(parts, heads, requests, group_size)
    return merge_last(sums, levels, last, requests, group_size)


def solution(mesh):
    in_specs = (
        P(("groups", "blk"), ("kv", "pair"), None),
        P(("groups", "blk", "pair"), "kv", None),
        P(("groups", "blk", "pair"), "kv", None),
        P(("groups", "blk"), "pair", "kv", None),
        P(("groups", "blk"), "pair", "kv", None),
        P(("groups", "blk")),
        P(("groups", "blk")),
    )
    out_specs = P(("groups", "blk"), ("kv", "pair"), None)
    return jax.shard_map(local, mesh=mesh, in_specs=in_specs, out_specs=out_specs, check_vma=False)
```

```python
import functools
import math

import jax
import jax.numpy as jnp
from jax import lax
from jax.experimental import pallas as pl
from jax.experimental.pallas import tpu as pltpu
from jax.sharding import PartitionSpec as P

masked_floor = -1e30
lowest_reference = -1e29
lane_count = 128
stat_pieces = 3
vmem_grant = 24 * 2**20
chunk_tokens = 256
least_total = 2.0**-60
most_total = 2.0**100


def vmem_spec():
    return pl.BlockSpec(memory_space=pltpu.VMEM)


def smem_spec():
    return pl.BlockSpec(memory_space=pltpu.SMEM)


def any_specs(operands):
    return [pl.BlockSpec(memory_space=pl.ANY)] * len(operands)


def ordered(kernel, after):
    return lambda *refs: kernel(*refs[len(after) :])


def light_cost():
    return pl.CostEstimate(flops=1, bytes_accessed=1, transcendentals=0)


def heavy_cost():
    return pl.CostEstimate(flops=10**10, bytes_accessed=1, transcendentals=0)


def kernel_params(grant=vmem_grant):
    return pltpu.CompilerParams(vmem_limit_bytes=grant)


def exchange(value, axis, apart):
    return lax.ppermute(value, axis, [(i, i ^ apart) for i in range(lax.axis_size(axis))])


def stat_rows(rows):
    return -(-stat_pieces * (rows // lane_count) // 16) * 16


def identity_mask():
    shape = (lane_count, lane_count)
    return lax.broadcasted_iota(jnp.int32, shape, 0) == lax.broadcasted_iota(jnp.int32, shape, 1)


def column_to_rows(column, same):
    pieces = []
    for start in range(0, column.shape[0], lane_count):
        wide = jnp.broadcast_to(column[start : start + lane_count], (lane_count, lane_count))
        pieces.append(jnp.sum(jnp.where(same, wide, 0.0), axis=0, keepdims=True))
    return pieces


def rows_to_column(pieces, same):
    columns = []
    for piece in pieces:
        wide = jnp.broadcast_to(piece, (lane_count, lane_count))
        columns.append(jnp.sum(jnp.where(same, wide, 0.0), axis=1, keepdims=True))
    return jnp.concatenate(columns, axis=0)


def split_stat(value):
    pieces = []
    for _ in range(stat_pieces):
        piece = value.astype(jnp.bfloat16)
        pieces.append(piece)
        value = value - piece.astype(jnp.float32)
    return pieces


def evaluate(pieces, scale, exact):
    state = None
    hidden = None
    for query, keys, values, limits in pieces:
        scores = lax.dot_general(
            query, keys, (((1,), (1,)), ((), ())), preferred_element_type=jnp.float32
        )
        seen = None
        if limits is not None:
            each = scores.shape[1] // len(limits)
            ends = [limit for limit in limits for _ in range(each // lane_count)]
            seen = lax.broadcasted_iota(jnp.int32, scores.shape, 1) < jnp.concatenate(ends, axis=1)
            counts = [limit - b * each for b, limit in enumerate(limits)]
            most = functools.reduce(jnp.maximum, counts)
            hidden = jnp.where(most > 0, 0.0, 1.0)[:, :1]
        if exact:
            if seen is not None:
                scores = jnp.where(seen, scores, masked_floor)
            largest = jnp.max(scores, axis=1, keepdims=True)
            if seen is not None:
                largest = jnp.maximum(largest, lowest_reference)
            weights = jnp.exp2((scores - largest) * scale)
            largest = largest * scale
        else:
            weights = jnp.exp2(scores * scale)
            if seen is not None:
                weights = jnp.where(seen, weights, 0.0)
        totals = jnp.sum(weights, axis=1, keepdims=True)
        sums = jnp.dot(weights.astype(jnp.bfloat16), values, preferred_element_type=jnp.float32)
        if state is None:
            state = (sums, totals, largest if exact else None)
        elif exact:
            top = jnp.maximum(state[2], largest)
            one, two = jnp.exp2(state[2] - top), jnp.exp2(largest - top)
            state = (state[0] * one + sums * two, state[1] * one + totals * two, top)
        else:
            state = (state[0] + sums, state[1] + totals, None)
    sums, totals, largest = state
    sound = jnp.where((totals > least_total) & (totals < most_total), 1.0, 0.0)
    if hidden is not None:
        sound = jnp.maximum(sound, hidden)
        totals = totals + hidden
    level = jnp.log2(totals)
    if exact:
        level = level + largest
    if hidden is not None:
        level = level + hidden * masked_floor
    return sums * (1.0 / totals), level, sound


def combine(parts):
    top = parts[0][1]
    for _, level in parts[1:]:
        top = jnp.maximum(top, level)
    sums = totals = 0.0
    for out, level in parts:
        weight = jnp.exp2(level - top)
        sums = sums + out * weight
        totals = totals + weight
    return sums * (1.0 / totals), top + jnp.log2(totals)


def write_partials(jobs, scale, heads, requests, group_size, others=()):
    same = identity_mask()

    loaded = [load_packed(ref, heads, requests, group_size, same) for ref in others]

    def run(exact):
        least = 1.0
        for out_ref, pieces_of in jobs:
            outs, levels = [], []
            for h in range(heads):
                out, level, sound = evaluate(pieces_of(h), scale, exact)
                if others:
                    added = [(o[h], l[h]) for o, l in loaded]
                    out, level = combine([(out, level), *added])
                outs.append(out)
                levels.append(level)
                least = jnp.minimum(least, sound)
            store_packed(out_ref, heads, requests, group_size, outs, levels, same)
        return jnp.min(least)

    least = run(False)

    @pl.when(least < 0.5)
    def _():
        run(True)


def store_packed(out_ref, heads, requests, group_size, outs, levels, same):
    rows = requests * heads * group_size
    per_head = requests * group_size
    all_rows = []
    for h in range(heads):
        block = outs[h].astype(jnp.bfloat16).reshape(requests, group_size, lane_count)
        for r in range(requests):
            out_ref[pl.ds((r * heads + h) * group_size, group_size), :] = block[r]
        all_rows += column_to_rows(levels[h], same)
    stats = jnp.concatenate(all_rows, axis=0)
    pieces = [piece.astype(jnp.float32) for piece in split_stat(stats)]
    spare = stat_rows(rows) - stat_pieces * stats.shape[0]
    if spare:
        pieces.append(jnp.zeros((spare, lane_count), jnp.float32))
    out_ref[pl.ds(rows, stat_rows(rows)), :] = jnp.concatenate(pieces, axis=0).astype(jnp.bfloat16)


def load_packed(in_ref, heads, requests, group_size, same):
    rows = requests * heads * group_size
    lines = rows // lane_count
    per_head = lines // heads
    stats = in_ref[pl.ds(rows, stat_rows(rows)), :].astype(jnp.float32)
    joined = stats[:lines]
    for piece in range(1, stat_pieces):
        joined = joined + stats[piece * lines : (piece + 1) * lines]
    outs, levels = [], []
    for h in range(heads):
        parts = [
            in_ref[pl.ds((r * heads + h) * group_size, group_size), :] for r in range(requests)
        ]
        outs.append(jnp.concatenate(parts, axis=0).astype(jnp.float32))
        lines_here = [joined[h * per_head + i : h * per_head + i + 1] for i in range(per_head)]
        levels.append(rows_to_column(lines_here, same))
    return outs, levels


def head_queries(query_ref, head, group_size):
    block = query_ref[:, head * group_size : (head + 1) * group_size, :]
    return block.reshape(block.shape[0] * group_size, block.shape[2])


def split_heads(source_ref, target_ref, wide_ref, shared, first, heads, base):
    tokens = source_ref.shape[0] // shared
    chunk = wide_ref.shape[0] // shared

    @pl.loop(0, tokens // chunk)
    def _(step):
        start = pl.multiple_of(step * chunk, chunk)
        rows = pl.multiple_of(step * (chunk * shared), chunk * shared)
        wide_ref[...] = source_ref[pl.ds(rows, chunk * shared), :].astype(jnp.float32)
        for h in range(heads):
            picked = wide_ref[pl.ds(first + h, chunk, stride=shared), :]
            target_ref[h, pl.ds(base + start, chunk), :] = picked.astype(target_ref.dtype)


def flat(cache):
    *lead, tokens, shared, width = cache.shape
    return cache.reshape(*lead, tokens * shared, width)


def packed_shape(query):
    requests, local_heads, width = query.shape
    rows = requests * local_heads
    return jax.ShapeDtypeStruct((rows + stat_rows(rows), width), query.dtype)


def root_pieces(query_ref, k_ref, v_ref, group_size):
    return lambda h: [(head_queries(query_ref, h, group_size), k_ref[h], v_ref[h], None)]


def first_kernel(
    scale, shared, query_ref, ko_ref, vo_ref, kp_ref, vp_ref, k_ref, v_ref, out_ref, wide_ref
):
    heads, both, _ = k_ref.shape
    first = lax.axis_index("pair") * heads
    for base, keys, values in ((0, ko_ref, vo_ref), (both // 2, kp_ref, vp_ref)):
        split_heads(keys, k_ref, wide_ref, shared, first, heads, base)
        split_heads(values, v_ref, wide_ref, shared, first, heads, base)
    requests, local_heads, _ = query_ref.shape
    group_size = local_heads // heads
    pieces = root_pieces(query_ref, k_ref, v_ref, group_size)
    write_partials([(out_ref, pieces)], scale, heads, requests, group_size)


def first_block(query, keys, values, other_keys, other_values, scale, heads, after):
    tokens, shared, width = keys.shape
    shape = jax.ShapeDtypeStruct((heads, 2 * tokens, width), keys.dtype)
    return pl.pallas_call(
        ordered(functools.partial(first_kernel, scale, shared), after),
        out_shape=(shape, shape, packed_shape(query)),
        in_specs=any_specs(after) + [vmem_spec()] * 5,
        out_specs=(vmem_spec(),) * 3,
        scratch_shapes=[pltpu.VMEM((chunk_tokens * shared, width), jnp.float32)],
        compiler_params=kernel_params(),
        cost_estimate=light_cost(),
        name="first_block",
    )(*after, query, flat(keys), flat(values), flat(other_keys), flat(other_values))


def limits_kernel(tokens, group_size, branch_ref, seen_ref, limit_ref):
    branches = limit_ref.shape[0]
    before = lax.axis_index("pair") * tokens
    for b in range(branches):
        for r in range(branch_ref.shape[0]):
            here = branch_ref[r] % branches == b
            count = jnp.clip(seen_ref[r] - before, 0, tokens)
            limit = b * tokens + jnp.where(here, count, 0)
            limit_ref[b, pl.ds(r * group_size, group_size), :] = jnp.full(
                (group_size, lane_count), limit, jnp.int32
            )


def limits_block(branch, seen, branches, tokens, group_size, after):
    shape = (branches, branch.shape[0] * group_size, lane_count)
    return pl.pallas_call(
        ordered(functools.partial(limits_kernel, tokens, group_size), after),
        out_shape=jax.ShapeDtypeStruct(shape, jnp.int32),
        in_specs=any_specs(after) + [smem_spec()] * 2,
        out_specs=vmem_spec(),
        compiler_params=kernel_params(2**20),
        cost_estimate=light_cost(),
        name="limits_block",
    )(*after, branch, seen)


def mark_kernel(out_ref):
    out_ref[...] = jnp.zeros_like(out_ref)


def mark():
    return pl.pallas_call(
        mark_kernel,
        out_shape=jax.ShapeDtypeStruct((8, lane_count), jnp.float32),
        out_specs=vmem_spec(),
        compiler_params=kernel_params(2**20),
        cost_estimate=heavy_cost(),
        name="mark",
    )()


def root_kernel(scale, count, k_ref, v_ref, *refs):
    heads = k_ref.shape[0]
    requests, local_heads, _ = refs[0].shape
    group_size = local_heads // heads
    jobs = [
        (out_ref, root_pieces(query_ref, k_ref, v_ref, group_size))
        for query_ref, out_ref in zip(refs[:count], refs[count:])
    ]
    write_partials(jobs, scale, heads, requests, group_size)


def head_kernel(scale, head, k_ref, v_ref, query_ref, out_ref):
    requests, local_heads, _ = query_ref.shape
    group_size = local_heads // k_ref.shape[0]
    pieces = root_pieces(query_ref, k_ref, v_ref, group_size)
    write_partials([(out_ref, lambda _: pieces(head))], scale, 1, requests, group_size)


def head_block(head, query, keys, values, scale, after):
    requests, local_heads, width = query.shape
    rows = requests * local_heads // keys.shape[0]
    return pl.pallas_call(
        ordered(functools.partial(head_kernel, scale, head), after),
        out_shape=jax.ShapeDtypeStruct((rows + stat_rows(rows), width), query.dtype),
        in_specs=any_specs(after) + [vmem_spec()] * 3,
        out_specs=vmem_spec(),
        compiler_params=kernel_params(),
        cost_estimate=light_cost(),
        name="head_block",
    )(*after, keys, values, query)


def root_blocks(queries, keys, values, scale, after):
    return pl.pallas_call(
        ordered(functools.partial(root_kernel, scale, len(queries)), after),
        out_shape=[packed_shape(query) for query in queries],
        in_specs=any_specs(after) + [vmem_spec()] * (2 + len(queries)),
        out_specs=[vmem_spec()] * len(queries),
        compiler_params=kernel_params(),
        cost_estimate=light_cost(),
        name="root_blocks",
    )(*after, keys, values, *queries)


def branch_pieces(query_ref, k_ref, v_ref, limit_ref, owner, heads, group_size):
    def pieces(h):
        at = owner * heads + h
        limits = [limit_ref[b] for b in range(limit_ref.shape[0])]
        return [(head_queries(query_ref, h, group_size), k_ref[at], v_ref[at], limits)]

    return pieces


def theirs_kernel(
    scale, heads, limit_ref, query_ref, bk_ref, bv_ref, out_ref, k_ref, v_ref, wide_ref
):
    requests, local_heads, _ = query_ref.shape
    shared, slots, _ = k_ref.shape
    branches = bk_ref.shape[0]
    group_size = local_heads // heads
    for b in range(branches):
        base = b * (slots // branches)
        split_heads(bk_ref.at[b], k_ref, wide_ref, shared, 0, shared, base)
        split_heads(bv_ref.at[b], v_ref, wide_ref, shared, 0, shared, base)
    owner = 1 - lax.axis_index("pair")
    pieces = branch_pieces(query_ref, k_ref, v_ref, limit_ref, owner, heads, group_size)
    write_partials([(out_ref, pieces)], scale, heads, requests, group_size)


def mine_kernel(scale, heads, limit_ref, query_ref, k_ref, v_ref, *refs):
    *others, out_ref = refs
    requests, local_heads, _ = query_ref.shape
    group_size = local_heads // heads
    owner = lax.axis_index("pair")
    pieces = branch_pieces(query_ref, k_ref, v_ref, limit_ref, owner, heads, group_size)
    write_partials([(out_ref, pieces)], scale, heads, requests, group_size, others)


def theirs_block(limits, query, keys, values, scale, heads, after):
    branches, tokens, shared, width = keys.shape
    held = jax.ShapeDtypeStruct((shared, branches * tokens, width), keys.dtype)
    return pl.pallas_call(
        ordered(functools.partial(theirs_kernel, scale, heads), after),
        out_shape=(packed_shape(query), held, held),
        in_specs=any_specs(after) + [vmem_spec()] * 4,
        out_specs=(vmem_spec(),) * 3,
        scratch_shapes=[pltpu.VMEM((chunk_tokens * shared, width), jnp.float32)],
        compiler_params=kernel_params(),
        cost_estimate=light_cost(),
        name="theirs_block",
    )(*after, limits, query, flat(keys), flat(values))


def mine_block(limits, query, keys, values, others, scale, heads, after):
    return pl.pallas_call(
        ordered(functools.partial(mine_kernel, scale, heads), after),
        out_shape=packed_shape(query),
        in_specs=any_specs(after) + [vmem_spec()] * (4 + len(others)),
        out_specs=vmem_spec(),
        compiler_params=kernel_params(),
        cost_estimate=heavy_cost(),
        name="mine_block",
    )(*after, limits, query, keys, values, *others)


def gather_kernel(requests, group_size, whole, *refs):
    *ins, sums_ref, level_ref = refs
    heads = sums_ref.shape[0]
    same = identity_mask()
    loaded = [load_packed(ref, heads, requests, group_size, same) for ref in ins[:whole]]
    for at in range(whole, len(ins), heads):
        ones = [load_packed(ref, 1, requests, group_size, same) for ref in ins[at : at + heads]]
        loaded.append(([o[0] for o, _ in ones], [l[0] for _, l in ones]))
    for h in range(heads):
        out, level = combine([(o[h], l[h]) for o, l in loaded])
        sums_ref[h] = out
        level_ref[h] = jnp.broadcast_to(level, out.shape)


def gather_partials(parts, halves, heads, requests, group_size):
    shape = jax.ShapeDtypeStruct((heads, requests * group_size, lane_count), jnp.float32)
    return pl.pallas_call(
        functools.partial(gather_kernel, requests, group_size, len(parts)),
        out_shape=(shape, shape),
        in_specs=[vmem_spec()] * (len(parts) + len(halves)),
        out_specs=(vmem_spec(), vmem_spec()),
        compiler_params=kernel_params(),
        cost_estimate=light_cost(),
        name="gather_partials",
    )(*parts, *halves)


def last_kernel(requests, group_size, sums_ref, level_ref, back_ref, out_ref):
    heads = sums_ref.shape[0]
    outs, levels = load_packed(back_ref, heads, requests, group_size, identity_mask())
    for h in range(heads):
        parts = [(sums_ref[h], level_ref[h]), (outs[h], levels[h])]
        out, _ = combine(parts)
        block = out.astype(out_ref.dtype).reshape(requests, group_size, lane_count)
        out_ref[:, h * group_size : (h + 1) * group_size, :] = block


def merge_last(sums, levels, back, requests, group_size):
    shape = (requests, sums.shape[0] * group_size, lane_count)
    return pl.pallas_call(
        functools.partial(last_kernel, requests, group_size),
        out_shape=jax.ShapeDtypeStruct(shape, back.dtype),
        in_specs=[vmem_spec()] * 3,
        out_specs=vmem_spec(),
        compiler_params=kernel_params(),
        cost_estimate=light_cost(),
        name="merge_last",
    )(sums, levels, back)


def local(queries, root_keys, root_values, branch_keys, branch_values, request_branch, seen_tokens):
    requests, local_heads, width = queries.shape
    shared = root_keys.shape[1]
    blocks = lax.axis_size("blk")
    heads = shared // lax.axis_size("pair")
    group_size = local_heads // heads
    scale = math.log2(math.e) / math.sqrt(width)

    other_keys = exchange(root_keys, "pair", 1)
    other_values = exchange(root_values, "pair", 1)
    other_queries = exchange(queries, "pair", 1)
    direct = range(blocks - 1, 0, -2)
    arrived = {apart: exchange(queries, "blk", apart) for apart in direct}

    keys, values, own = first_block(
        queries, root_keys, root_values, other_keys, other_values, scale, heads, (mark(),)
    )
    groups = [(apart, apart ^ 1) for apart in direct if apart > 1]
    for far, near in groups:
        arrived[far], own = lax.optimization_barrier((arrived[far], own))
        arrived[near] = exchange(arrived[far], "blk", 1)
    order = sorted(arrived, key=lambda apart: (apart % 2 == 0, -apart))
    returned, halves, previous = {}, [], ()
    for apart in order:
        if apart > 2 and apart % 2:
            for head in range(heads):
                previous = (head_block(head, arrived[apart], keys, values, scale, previous),)
                halves.append(exchange(previous[0], "blk", apart))
            continue
        previous = root_blocks([arrived[apart]], keys, values, scale, previous)
        returned[apart] = exchange(previous[0], "blk", apart)
    branches, tokens, _, _ = branch_keys.shape
    limits = limits_block(
        request_branch, seen_tokens, branches, tokens, group_size, previous
    )
    theirs, held_keys, held_values = theirs_block(
        limits, other_queries, branch_keys, branch_values, scale, heads, previous
    )
    from_partner = exchange(theirs, "pair", 1)
    mine = mine_block(limits, queries, held_keys, held_values, [own], scale, heads, halves[:1])
    last = returned.pop(order[-1])
    parts = [mine, from_partner, *returned.values()]
    sums, levels = gather_partials(parts, halves, heads, requests, group_size)
    return merge_last(sums, levels, last, requests, group_size)


def solution(mesh):
    in_specs = (
        P(("groups", "blk"), ("kv", "pair"), None),
        P(("groups", "blk", "pair"), "kv", None),
        P(("groups", "blk", "pair"), "kv", None),
        P(("groups", "blk"), "pair", "kv", None),
        P(("groups", "blk"), "pair", "kv", None),
        P(("groups", "blk")),
        P(("groups", "blk")),
    )
    out_specs = P(("groups", "blk"), ("kv", "pair"), None)
    return jax.shard_map(local, mesh=mesh, in_specs=in_specs, out_specs=out_specs, check_vma=False)
```

```python
import functools
import math

import jax
import jax.numpy as jnp
from jax import lax
from jax.experimental import pallas as pl
from jax.experimental.pallas import tpu as pltpu
from jax.sharding import PartitionSpec as P

masked_floor = -1e30
lowest_reference = -1e29
lane_count = 128
stat_pieces = 3
vmem_grant = 24 * 2**20
chunk_tokens = 256
least_total = 2.0**-60
most_total = 2.0**100


def vmem_spec():
    return pl.BlockSpec(memory_space=pltpu.VMEM)


def smem_spec():
    return pl.BlockSpec(memory_space=pltpu.SMEM)


def any_specs(operands):
    return [pl.BlockSpec(memory_space=pl.ANY)] * len(operands)


def ordered(kernel, after):
    return lambda *refs: kernel(*refs[len(after) :])


def light_cost():
    return pl.CostEstimate(flops=1, bytes_accessed=1, transcendentals=0)


def heavy_cost():
    return pl.CostEstimate(flops=10**10, bytes_accessed=1, transcendentals=0)


def kernel_params(grant=vmem_grant):
    return pltpu.CompilerParams(vmem_limit_bytes=grant)


def exchange(value, axis, apart):
    return lax.ppermute(value, axis, [(i, i ^ apart) for i in range(lax.axis_size(axis))])


def stat_rows(rows):
    return -(-stat_pieces * (rows // lane_count) // 16) * 16


def identity_mask():
    shape = (lane_count, lane_count)
    return lax.broadcasted_iota(jnp.int32, shape, 0) == lax.broadcasted_iota(jnp.int32, shape, 1)


def column_to_rows(column, same):
    pieces = []
    for start in range(0, column.shape[0], lane_count):
        wide = jnp.broadcast_to(column[start : start + lane_count], (lane_count, lane_count))
        pieces.append(jnp.sum(jnp.where(same, wide, 0.0), axis=0, keepdims=True))
    return pieces


def rows_to_column(pieces, same):
    columns = []
    for piece in pieces:
        wide = jnp.broadcast_to(piece, (lane_count, lane_count))
        columns.append(jnp.sum(jnp.where(same, wide, 0.0), axis=1, keepdims=True))
    return jnp.concatenate(columns, axis=0)


def split_stat(value):
    pieces = []
    for _ in range(stat_pieces):
        piece = value.astype(jnp.bfloat16)
        pieces.append(piece)
        value = value - piece.astype(jnp.float32)
    return pieces


def evaluate(pieces, scale, exact):
    state = None
    hidden = None
    for query, keys, values, limits in pieces:
        scores = lax.dot_general(
            query, keys, (((1,), (1,)), ((), ())), preferred_element_type=jnp.float32
        )
        seen = None
        if limits is not None:
            each = scores.shape[1] // len(limits)
            ends = [limit for limit in limits for _ in range(each // lane_count)]
            seen = lax.broadcasted_iota(jnp.int32, scores.shape, 1) < jnp.concatenate(ends, axis=1)
            counts = [limit - b * each for b, limit in enumerate(limits)]
            most = functools.reduce(jnp.maximum, counts)
            hidden = jnp.where(most > 0, 0.0, 1.0)[:, :1]
        if exact:
            if seen is not None:
                scores = jnp.where(seen, scores, masked_floor)
            largest = jnp.max(scores, axis=1, keepdims=True)
            if seen is not None:
                largest = jnp.maximum(largest, lowest_reference)
            weights = jnp.exp2((scores - largest) * scale)
            largest = largest * scale
        else:
            weights = jnp.exp2(scores * scale)
            if seen is not None:
                weights = jnp.where(seen, weights, 0.0)
        totals = jnp.sum(weights, axis=1, keepdims=True)
        sums = jnp.dot(weights.astype(jnp.bfloat16), values, preferred_element_type=jnp.float32)
        if state is None:
            state = (sums, totals, largest if exact else None)
        elif exact:
            top = jnp.maximum(state[2], largest)
            one, two = jnp.exp2(state[2] - top), jnp.exp2(largest - top)
            state = (state[0] * one + sums * two, state[1] * one + totals * two, top)
        else:
            state = (state[0] + sums, state[1] + totals, None)
    sums, totals, largest = state
    sound = jnp.where((totals > least_total) & (totals < most_total), 1.0, 0.0)
    if hidden is not None:
        sound = jnp.maximum(sound, hidden)
        totals = totals + hidden
    level = jnp.log2(totals)
    if exact:
        level = level + largest
    if hidden is not None:
        level = level + hidden * masked_floor
    return sums * (1.0 / totals), level, sound


def combine(parts):
    top = parts[0][1]
    for _, level in parts[1:]:
        top = jnp.maximum(top, level)
    sums = totals = 0.0
    for out, level in parts:
        weight = jnp.exp2(level - top)
        sums = sums + out * weight
        totals = totals + weight
    return sums * (1.0 / totals), top + jnp.log2(totals)


def write_partials(jobs, scale, heads, requests, group_size, others=()):
    same = identity_mask()

    loaded = [load_packed(ref, heads, requests, group_size, same) for ref in others]

    def run(exact):
        least = 1.0
        for out_ref, pieces_of in jobs:
            outs, levels = [], []
            for h in range(heads):
                out, level, sound = evaluate(pieces_of(h), scale, exact)
                if others:
                    added = [(o[h], l[h]) for o, l in loaded]
                    out, level = combine([(out, level), *added])
                outs.append(out)
                levels.append(level)
                least = jnp.minimum(least, sound)
            store_packed(out_ref, heads, requests, group_size, outs, levels, same)
        return jnp.min(least)

    least = run(False)

    @pl.when(least < 0.5)
    def _():
        run(True)


def store_packed(out_ref, heads, requests, group_size, outs, levels, same):
    rows = requests * heads * group_size
    per_head = requests * group_size
    all_rows = []
    for h in range(heads):
        block = outs[h].astype(jnp.bfloat16).reshape(requests, group_size, lane_count)
        for r in range(requests):
            out_ref[pl.ds((r * heads + h) * group_size, group_size), :] = block[r]
        all_rows += column_to_rows(levels[h], same)
    stats = jnp.concatenate(all_rows, axis=0)
    pieces = [piece.astype(jnp.float32) for piece in split_stat(stats)]
    spare = stat_rows(rows) - stat_pieces * stats.shape[0]
    if spare:
        pieces.append(jnp.zeros((spare, lane_count), jnp.float32))
    out_ref[pl.ds(rows, stat_rows(rows)), :] = jnp.concatenate(pieces, axis=0).astype(jnp.bfloat16)


def load_packed(in_ref, heads, requests, group_size, same):
    rows = requests * heads * group_size
    lines = rows // lane_count
    per_head = lines // heads
    stats = in_ref[pl.ds(rows, stat_rows(rows)), :].astype(jnp.float32)
    joined = stats[:lines]
    for piece in range(1, stat_pieces):
        joined = joined + stats[piece * lines : (piece + 1) * lines]
    outs, levels = [], []
    for h in range(heads):
        parts = [
            in_ref[pl.ds((r * heads + h) * group_size, group_size), :] for r in range(requests)
        ]
        outs.append(jnp.concatenate(parts, axis=0).astype(jnp.float32))
        lines_here = [joined[h * per_head + i : h * per_head + i + 1] for i in range(per_head)]
        levels.append(rows_to_column(lines_here, same))
    return outs, levels


def head_queries(query_ref, head, group_size):
    block = query_ref[:, head * group_size : (head + 1) * group_size, :]
    return block.reshape(block.shape[0] * group_size, block.shape[2])


def split_heads(source_ref, target_ref, wide_ref, shared, first, heads, base):
    tokens = source_ref.shape[0] // shared
    chunk = wide_ref.shape[0] // shared

    @pl.loop(0, tokens // chunk)
    def _(step):
        start = pl.multiple_of(step * chunk, chunk)
        rows = pl.multiple_of(step * (chunk * shared), chunk * shared)
        wide_ref[...] = source_ref[pl.ds(rows, chunk * shared), :].astype(jnp.float32)
        for h in range(heads):
            picked = wide_ref[pl.ds(first + h, chunk, stride=shared), :]
            target_ref[h, pl.ds(base + start, chunk), :] = picked.astype(target_ref.dtype)


def flat(cache):
    *lead, tokens, shared, width = cache.shape
    return cache.reshape(*lead, tokens * shared, width)


def packed_shape(query):
    requests, local_heads, width = query.shape
    rows = requests * local_heads
    return jax.ShapeDtypeStruct((rows + stat_rows(rows), width), query.dtype)


def root_pieces(query_ref, k_ref, v_ref, group_size):
    return lambda h: [(head_queries(query_ref, h, group_size), k_ref[h], v_ref[h], None)]


def first_kernel(
    scale, shared, query_ref, ko_ref, vo_ref, kp_ref, vp_ref, k_ref, v_ref, out_ref, wide_ref
):
    heads, both, _ = k_ref.shape
    first = lax.axis_index("pair") * heads
    for base, keys, values in ((0, ko_ref, vo_ref), (both // 2, kp_ref, vp_ref)):
        split_heads(keys, k_ref, wide_ref, shared, first, heads, base)
        split_heads(values, v_ref, wide_ref, shared, first, heads, base)
    requests, local_heads, _ = query_ref.shape
    group_size = local_heads // heads
    pieces = root_pieces(query_ref, k_ref, v_ref, group_size)
    write_partials([(out_ref, pieces)], scale, heads, requests, group_size)


def first_block(query, keys, values, other_keys, other_values, scale, heads, after):
    tokens, shared, width = keys.shape
    shape = jax.ShapeDtypeStruct((heads, 2 * tokens, width), keys.dtype)
    return pl.pallas_call(
        ordered(functools.partial(first_kernel, scale, shared), after),
        out_shape=(shape, shape, packed_shape(query)),
        in_specs=any_specs(after) + [vmem_spec()] * 5,
        out_specs=(vmem_spec(),) * 3,
        scratch_shapes=[pltpu.VMEM((chunk_tokens * shared, width), jnp.float32)],
        compiler_params=kernel_params(),
        cost_estimate=light_cost(),
        name="first_block",
    )(*after, query, flat(keys), flat(values), flat(other_keys), flat(other_values))


def limits_kernel(tokens, group_size, branch_ref, seen_ref, limit_ref):
    branches = limit_ref.shape[0]
    before = lax.axis_index("pair") * tokens
    for b in range(branches):
        for r in range(branch_ref.shape[0]):
            here = branch_ref[r] % branches == b
            count = jnp.clip(seen_ref[r] - before, 0, tokens)
            limit = b * tokens + jnp.where(here, count, 0)
            limit_ref[b, pl.ds(r * group_size, group_size), :] = jnp.full(
                (group_size, lane_count), limit, jnp.int32
            )


def limits_block(branch, seen, branches, tokens, group_size, after):
    shape = (branches, branch.shape[0] * group_size, lane_count)
    return pl.pallas_call(
        ordered(functools.partial(limits_kernel, tokens, group_size), after),
        out_shape=jax.ShapeDtypeStruct(shape, jnp.int32),
        in_specs=any_specs(after) + [smem_spec()] * 2,
        out_specs=vmem_spec(),
        compiler_params=kernel_params(2**20),
        cost_estimate=light_cost(),
        name="limits_block",
    )(*after, branch, seen)


def mark_kernel(out_ref):
    out_ref[...] = jnp.zeros_like(out_ref)


def mark():
    return pl.pallas_call(
        mark_kernel,
        out_shape=jax.ShapeDtypeStruct((8, lane_count), jnp.float32),
        out_specs=vmem_spec(),
        compiler_params=kernel_params(2**20),
        cost_estimate=heavy_cost(),
        name="mark",
    )()


def root_kernel(scale, count, k_ref, v_ref, *refs):
    heads = k_ref.shape[0]
    requests, local_heads, _ = refs[0].shape
    group_size = local_heads // heads
    jobs = [
        (out_ref, root_pieces(query_ref, k_ref, v_ref, group_size))
        for query_ref, out_ref in zip(refs[:count], refs[count:])
    ]
    write_partials(jobs, scale, heads, requests, group_size)


def root_blocks(queries, keys, values, scale, after):
    return pl.pallas_call(
        ordered(functools.partial(root_kernel, scale, len(queries)), after),
        out_shape=[packed_shape(query) for query in queries],
        in_specs=any_specs(after) + [vmem_spec()] * (2 + len(queries)),
        out_specs=[vmem_spec()] * len(queries),
        compiler_params=kernel_params(),
        cost_estimate=light_cost(),
        name="root_blocks",
    )(*after, keys, values, *queries)


def branch_pieces(query_ref, k_ref, v_ref, limit_ref, owner, heads, group_size):
    def pieces(h):
        at = owner * heads + h
        limits = [limit_ref[b] for b in range(limit_ref.shape[0])]
        return [(head_queries(query_ref, h, group_size), k_ref[at], v_ref[at], limits)]

    return pieces


def theirs_kernel(
    scale, heads, limit_ref, query_ref, bk_ref, bv_ref, out_ref, k_ref, v_ref, wide_ref
):
    requests, local_heads, _ = query_ref.shape
    shared, slots, _ = k_ref.shape
    branches = bk_ref.shape[0]
    group_size = local_heads // heads
    for b in range(branches):
        base = b * (slots // branches)
        split_heads(bk_ref.at[b], k_ref, wide_ref, shared, 0, shared, base)
        split_heads(bv_ref.at[b], v_ref, wide_ref, shared, 0, shared, base)
    owner = 1 - lax.axis_index("pair")
    pieces = branch_pieces(query_ref, k_ref, v_ref, limit_ref, owner, heads, group_size)
    write_partials([(out_ref, pieces)], scale, heads, requests, group_size)


def mine_kernel(scale, heads, limit_ref, query_ref, k_ref, v_ref, *refs):
    *others, out_ref = refs
    requests, local_heads, _ = query_ref.shape
    group_size = local_heads // heads
    owner = lax.axis_index("pair")
    pieces = branch_pieces(query_ref, k_ref, v_ref, limit_ref, owner, heads, group_size)
    write_partials([(out_ref, pieces)], scale, heads, requests, group_size, others)


def theirs_block(limits, query, keys, values, scale, heads, after):
    branches, tokens, shared, width = keys.shape
    held = jax.ShapeDtypeStruct((shared, branches * tokens, width), keys.dtype)
    return pl.pallas_call(
        ordered(functools.partial(theirs_kernel, scale, heads), after),
        out_shape=(packed_shape(query), held, held),
        in_specs=any_specs(after) + [vmem_spec()] * 4,
        out_specs=(vmem_spec(),) * 3,
        scratch_shapes=[pltpu.VMEM((chunk_tokens * shared, width), jnp.float32)],
        compiler_params=kernel_params(),
        cost_estimate=light_cost(),
        name="theirs_block",
    )(*after, limits, query, flat(keys), flat(values))


def mine_block(limits, query, keys, values, others, scale, heads):
    return pl.pallas_call(
        functools.partial(mine_kernel, scale, heads),
        out_shape=packed_shape(query),
        in_specs=[vmem_spec()] * (4 + len(others)),
        out_specs=vmem_spec(),
        compiler_params=kernel_params(),
        cost_estimate=heavy_cost(),
        name="mine_block",
    )(limits, query, keys, values, *others)


def gather_kernel(requests, group_size, *refs):
    *ins, sums_ref, level_ref = refs
    heads = sums_ref.shape[0]
    same = identity_mask()
    loaded = [load_packed(ref, heads, requests, group_size, same) for ref in ins]
    for h in range(heads):
        out, level = combine([(o[h], l[h]) for o, l in loaded])
        sums_ref[h] = out
        level_ref[h] = jnp.broadcast_to(level, out.shape)


def gather_partials(parts, heads, requests, group_size):
    shape = jax.ShapeDtypeStruct((heads, requests * group_size, lane_count), jnp.float32)
    return pl.pallas_call(
        functools.partial(gather_kernel, requests, group_size),
        out_shape=(shape, shape),
        in_specs=[vmem_spec()] * len(parts),
        out_specs=(vmem_spec(), vmem_spec()),
        compiler_params=kernel_params(),
        cost_estimate=light_cost(),
        name="gather_partials",
    )(*parts)


def last_kernel(requests, group_size, sums_ref, level_ref, back_ref, out_ref):
    heads = sums_ref.shape[0]
    outs, levels = load_packed(back_ref, heads, requests, group_size, identity_mask())
    for h in range(heads):
        parts = [(sums_ref[h], level_ref[h]), (outs[h], levels[h])]
        out, _ = combine(parts)
        block = out.astype(out_ref.dtype).reshape(requests, group_size, lane_count)
        out_ref[:, h * group_size : (h + 1) * group_size, :] = block


def merge_last(sums, levels, back, requests, group_size):
    shape = (requests, sums.shape[0] * group_size, lane_count)
    return pl.pallas_call(
        functools.partial(last_kernel, requests, group_size),
        out_shape=jax.ShapeDtypeStruct(shape, back.dtype),
        in_specs=[vmem_spec()] * 3,
        out_specs=vmem_spec(),
        compiler_params=kernel_params(),
        cost_estimate=light_cost(),
        name="merge_last",
    )(sums, levels, back)


def local(queries, root_keys, root_values, branch_keys, branch_values, request_branch, seen_tokens):
    requests, local_heads, width = queries.shape
    shared = root_keys.shape[1]
    blocks = lax.axis_size("blk")
    heads = shared // lax.axis_size("pair")
    group_size = local_heads // heads
    scale = math.log2(math.e) / math.sqrt(width)

    other_keys = exchange(root_keys, "pair", 1)
    other_values = exchange(root_values, "pair", 1)
    other_queries = exchange(queries, "pair", 1)
    direct = range(blocks - 1, 0, -2)
    arrived = {apart: exchange(queries, "blk", apart) for apart in direct}

    keys, values, own = first_block(
        queries, root_keys, root_values, other_keys, other_values, scale, heads, (mark(),)
    )
    groups = [(apart, apart ^ 1) for apart in direct if apart > 1]
    for far, near in groups:
        arrived[far], own = lax.optimization_barrier((arrived[far], own))
        arrived[near] = exchange(arrived[far], "blk", 1)
    order = sorted(arrived, reverse=True)
    returned, previous = {}, ()
    for apart in order:
        previous = root_blocks([arrived[apart]], keys, values, scale, previous)
        returned[apart] = exchange(previous[0], "blk", apart)
    branches, tokens, _, _ = branch_keys.shape
    limits = limits_block(
        request_branch, seen_tokens, branches, tokens, group_size, previous
    )
    theirs, held_keys, held_values = theirs_block(
        limits, other_queries, branch_keys, branch_values, scale, heads, previous
    )
    from_partner = exchange(theirs, "pair", 1)
    mine = mine_block(limits, queries, held_keys, held_values, [own], scale, heads)
    last = returned.pop(min(order, key=lambda apart: abs(apart - 2)))
    parts = [mine, from_partner, *returned.values()]
    sums, levels = gather_partials(parts, heads, requests, group_size)
    return merge_last(sums, levels, last, requests, group_size)


def solution(mesh):
    in_specs = (
        P(("groups", "blk"), ("kv", "pair"), None),
        P(("groups", "blk", "pair"), "kv", None),
        P(("groups", "blk", "pair"), "kv", None),
        P(("groups", "blk"), "pair", "kv", None),
        P(("groups", "blk"), "pair", "kv", None),
        P(("groups", "blk")),
        P(("groups", "blk")),
    )
    out_specs = P(("groups", "blk"), ("kv", "pair"), None)
    return jax.shard_map(local, mesh=mesh, in_specs=in_specs, out_specs=out_specs, check_vma=False)
```
